128 devices in a mesh: px: 8 (over x, core), py: 16 (over z, y).
Axes of the slice: x: 4, y: 4, z: 4, core: 2. Of those that a mesh axis runs over, the one named last changes fastest.
Arguments:
- control_init: float32 [16, 1024, 1024], P(None, ('px', 'py')), may hold values from -3 to 3
- kernel_x: float32 [16, 64], replicated, may hold values from 0 to 0.25
- kernel_y: float32 [16, 64], replicated, may hold values from 0 to 0.25
- obs_weight: float32 [431], replicated, may hold values from 0.3 to 3
- jacobian: bfloat16 [16384, 16, 431], P(('px', 'py')), may hold values from -0.3125 to 0.3125
- innovation: bfloat16 [16384, 431], P(('px', 'py')), may hold values from -24 to 24
- obs_dest: int32 [16384, 1], P(('px', 'py')), may hold values from 0 to 127; in each aligned block of 128 rows (0 to 127, 128 to 255, ...) at most 2 rows name the same one
- obs_cell: int32 [16384], P(('px', 'py')), may hold values from 0 to 8191
Outputs:
- control: float32 [16, 1024, 1024], P(None, ('px', 'py'))
- residual: float32 [16, 1024, 1024], P(None, ('px', 'py'))
The draws below stay inside these ranges and needn't reach their ends.
Inputs may be any that keep to these rules, and one draw needn't show every extreme that they name: `obs_dest`: within the 128 rows of one device, no owner is named by more than 2 rows; some owner is named by exactly 2. `obs_cell`: column within the owner's block of 8 grid columns by 1024 rows, numbered local column * 1024 + row.
All inputs are finite; a program needn't handle non-finite values.
Results may differ from the reference program's by a relative error of at most 0.003.
Values may be sent and summed in bfloat16 or wider, within the bound.
A program may use at most 128 MiB of HBM per device.

```python
import math
import jax
import jax.numpy as jnp
import numpy as np
from jax import lax

LEV = 16
CH = 431
TAPS = 64
ITERS = 2
XC = 8
OB = 128
NX = 1024
NY = 1024
NOBS = 16384
CAP = 2
DEVICES = 128


def touch_ends(array, key, low, high):
    longest = array.shape.index(max(array.shape))
    spots = []
    for shift in (0, 1):
        where = [jax.random.randint(jax.random.fold_in(key, axis), (), 0, length) for axis, length in enumerate(array.shape)]
        where[longest] = (where[longest] + shift) % array.shape[longest]
        spots.append(tuple(where))
    return array.at[spots[0]].set(low).at[spots[1]].set(high)


def steps_of(stream_key, shape, shards, smallest, top_value):
    def one(axis_at, parts):
        draws = jax.random.uniform(jax.random.fold_in(jax.random.fold_in(stream_key, 6), axis_at), (parts,), jnp.float32, smallest / len(shards), top_value / len(shards))
        return jnp.repeat(jnp.exp(draws), shape[axis_at] // parts).reshape((-1,) + (1,) * (len(shape) - axis_at - 1))

    gain = one(*shards[0])
    for cut in shards[1:]:
        gain = gain * one(*cut)
    return gain


def assign_block(key, own, number, rows, count, top, limit, lean):
    order = jax.random.permutation(key, count)
    packed, common = portions_of(count, rows * top, limit, lean, True), portions_of(count, rows * top, limit, lean, False)
    places = jnp.arange(count)

    def named(sizes, turn):
        used = int((sizes > 0).sum())
        fixed = max(1, used // 4)
        passed = fixed + (places - fixed + turn * (used - fixed)) % max(1, count - fixed)
        return jnp.zeros((count,), jnp.int32).at[order[jnp.where(places < fixed, places, passed)]].set(jnp.asarray(sizes, jnp.int32))

    sizes = jnp.where(number % 4 == 0, named(packed, number // 4), named(common, number - number // 4 - 1))
    mixed = jax.random.permutation(jax.random.fold_in(own, 3), count)
    donor, receiver = mixed[0:count // 2 * 2:2], mixed[1:count // 2 * 2:2]
    slack = jnp.minimum(sizes[donor] - 1, limit - sizes[receiver]) // 2
    slack = jnp.where((donor == order[0]) | (receiver == order[0]) | (sizes[receiver] == 0), 0, jnp.maximum(slack, 0))
    passed = jax.random.randint(jax.random.fold_in(own, 4), (count // 2,), 0, 1 << 20) % (slack + 1)
    sizes = sizes.at[donor].add(-passed).at[receiver].add(passed)
    items = jnp.searchsorted(jnp.cumsum(sizes), jnp.arange(rows * top), side="right").astype(jnp.int32)
    listing = items.reshape(top, rows).T
    listing = listing[jax.random.permutation(jax.random.fold_in(own, 1), rows)]
    turn = jax.random.randint(jax.random.fold_in(own, 2), (rows, 1), 0, top)
    return jnp.take_along_axis(listing, (jnp.arange(top)[None, :] + turn) % top, axis=1)


def portions_of(count, total, most, skew, full):
    portions = [(1 << 20) // math.isqrt(standing ** skew) + 1 for standing in range(1, count + 1)]
    largest = most if full else min(most, max(-(-total // count), total * portions[0] // sum(portions)))
    least = 1 if total - largest >= count - 1 else 0
    given, rest = [largest] + [least] * (count - 1), total - largest - least * (count - 1)
    while rest > 0:
        movable = [i for i in range(1, count) if given[i] < largest] or [i for i in range(1, count) if given[i] < most]
        pool, remaining = sum([portions[i] for i in movable]), rest
        for i in movable:
            addition = min(most - given[i], max(1, remaining * portions[i] // pool), rest)
            given[i] = given[i] + addition
            rest = rest - addition
    return np.array(given)


def normal_values(stream_key, extent, scale, limit, split=(), kind=jnp.bfloat16):
    loudness = steps_of(stream_key, extent, split, -0.22, 0.18) if split else 1.0
    values = jax.random.normal(stream_key, extent, jnp.float32) * scale * loudness
    return jnp.minimum(jnp.maximum(values, -limit), limit).astype(kind)


def setup_inputs(seed: int = 0) -> dict:
    streams_of = jax.random.split(jax.random.key(seed), 9)
    control_init = normal_values(streams_of[0], (LEV, NY, NX), 0.5, 3.0, ((1, 128),), jnp.float32)
    kernel_x = jnp.clip(jax.random.uniform(streams_of[1], (LEV, TAPS), jnp.float32, 0.0, 0.25), 0.0, 0.25)
    kernel_y = jnp.clip(jax.random.uniform(streams_of[2], (LEV, TAPS), jnp.float32, 0.0, 0.25), 0.0, 0.25)
    obs_weight = jnp.clip(jnp.exp(jax.random.uniform(streams_of[3], (CH,), jnp.float32, math.log(0.3), math.log(3.0))), 0.3, 3.0)
    jacobian = normal_values(streams_of[4], (NOBS, LEV, CH), (LEV * CH // 16) ** -0.5, 0.3125, ((0, 128),))
    innovation = normal_values(streams_of[5], (NOBS, CH), 4.0, 24.0, ((0, 128),))
    obs_dest_keys = jax.random.split(jax.random.fold_in(streams_of[6], 1), NOBS // OB)
    obs_dest_turns = jax.random.permutation(jax.random.fold_in(streams_of[6], 3), NOBS // OB)
    obs_dest = jax.vmap(lambda own, number: assign_block(jax.random.fold_in(streams_of[6], 2), own, number, OB, DEVICES, 1, CAP, 2))(obs_dest_keys, obs_dest_turns).reshape((NOBS, 1))
    obs_cell = touch_ends(jax.random.randint(streams_of[7], (NOBS,), 0, XC * NY), jax.random.fold_in(streams_of[7], 1), 0, (XC * NY) - 1).astype(jnp.int32)
    return dict(control_init=control_init, kernel_x=kernel_x, kernel_y=kernel_y, obs_weight=obs_weight, jacobian=jacobian, innovation=innovation, obs_dest=obs_dest, obs_cell=obs_cell)


def band_table(kernel, flipped):
    tap_count = kernel.shape[1]
    window_len = 128 + tap_count
    row_index = jnp.arange(window_len, dtype=jnp.int32)[:, None, None]
    col_index = jnp.arange(128, dtype=jnp.int32)[None, :, None]
    tap_index = jnp.arange(tap_count, dtype=jnp.int32)[None, None, :]
    target = tap_count - tap_index if flipped else tap_index
    matches = (row_index - col_index == target).astype(jnp.float32)
    return jnp.einsum("jit,lt->lji", matches, kernel.astype(jnp.float32), precision=lax.Precision.HIGHEST)


def convolve(grid_field, banded, periodic, transposed):
    levels, row_count, length = grid_field.shape
    block_count = length // 128
    half_span = (banded.shape[1] - 128) // 2
    blocks = grid_field.reshape(levels, row_count, block_count, 128)
    before = jnp.roll(blocks, 1, axis=2)[..., 128 - half_span:]
    following = jnp.roll(blocks, -1, axis=2)[..., :half_span]
    if not periodic:
        block_index = jnp.arange(block_count, dtype=jnp.int32)
        before = before * (block_index > 0).astype(jnp.float32)[:, None]
        following = following * (block_index < block_count - 1).astype(jnp.float32)[:, None]
    window = jnp.concatenate([before, blocks, following], axis=3)
    if transposed:
        result = jnp.einsum("lrbj,lji->lbir", window, banded, precision=lax.Precision.HIGHEST)
        return result.reshape(levels, length, row_count)
    result = jnp.einsum("lrbj,lji->lrbi", window, banded, precision=lax.Precision.HIGHEST)
    return result.reshape(levels, row_count, length)


def observe(increment, jacobian, innovation, obs_weight, column, use_innovation):
    levels = increment.shape[0]
    flat_field = increment.reshape(levels, -1)
    profile = flat_field[:, column].T.astype(jnp.bfloat16)
    jac_wide = jacobian.astype(jnp.float32)
    evolved = jnp.einsum("olc,ol->oc", jac_wide, profile.astype(jnp.float32), precision=lax.Precision.HIGHEST)
    if use_innovation:
        evolved = evolved - innovation.astype(jnp.float32)
    weighted = (obs_weight[None, :] * evolved).astype(jnp.bfloat16)
    adjoint_rows = jnp.einsum("olc,oc->ol", jac_wide, weighted.astype(jnp.float32), precision=lax.Precision.HIGHEST)
    result = jnp.zeros_like(flat_field).at[:, column].add(adjoint_rows.T)
    return result.reshape(increment.shape)


def reference(control_init, kernel_x, kernel_y, obs_weight, jacobian, innovation, obs_dest, obs_cell):
    forward_x = band_table(kernel_x, False)
    forward_y = band_table(kernel_y, False)
    backward_x = band_table(kernel_x, True)
    backward_y = band_table(kernel_y, True)
    column = (obs_dest[:, 0] * (XC * NY) + obs_cell).astype(jnp.int32)

    def spread(values):
        return convolve(convolve(values, forward_x, True, True), forward_y, False, False)

    def gather_back(values):
        return convolve(convolve(values, backward_y, False, True), backward_x, True, False)

    gradient = control_init + gather_back(observe(spread(control_init), jacobian, innovation, obs_weight, column, True))
    residual = -gradient
    direction = residual
    control = control_init
    norm_now = jnp.sum(residual * residual)
    for iteration in range(ITERS):
        image = direction + gather_back(observe(spread(direction), jacobian, innovation, obs_weight, column, False))
        alpha = norm_now / jnp.sum(direction * image)
        control = control + alpha * direction
        residual = residual - alpha * image
        norm_next = jnp.sum(residual * residual)
        direction = residual + (norm_next / norm_now) * direction
        norm_now = norm_next
    return control, residual
```

```python
import functools

import jax
import jax.numpy as jnp
from jax import lax
from jax.experimental import pallas as pl
from jax.experimental.pallas import tpu as pltpu
from jax.sharding import PartitionSpec as P

F32, BF16, I32 = jnp.float32, jnp.bfloat16, jnp.int32
MESH = pl.DeviceIdType.MESH
ND, NPX, NPY = 128, 8, 16
LEV, CH, TAPS = 16, 431, 64
NEAR = 17
MIDDLE = 8
FX, BX, FY, BY = range(4)
NT = (((1,), (1,)), ((), ()))
NN = (((1,), (0,)), ((), ()))
HIGHEST = lax.Precision.HIGHEST


def iota(shape, axis):
    return lax.broadcasted_iota(I32, shape, axis)


def split(values):
    high = values.astype(BF16)
    low = (values - high.astype(F32)).astype(BF16)
    return high, low


def stacked(values):
    return jnp.concatenate(split(values), axis=0)


def dot(left, right, dims=NN, precision=None):
    return lax.dot_general(left, right, dims, precision=precision, preferred_element_type=F32)


def swap_groups(tiles):
    group = iota((8, 128), 1) // 8
    tiles = list(tiles)
    for bit in range(4):
        step = 1 << bit
        upper = (group & step) != 0
        for a in range(16):
            if a & step == 0:
                first, second = tiles[a], tiles[a + step]
                tiles[a] = jnp.where(upper, pltpu.roll(second, 8 * step, 1), first)
                tiles[a + step] = jnp.where(upper, second, pltpu.roll(first, 128 - 8 * step, 1))
    return tiles


def spread_levels(values):
    count = values.shape[1]
    return jnp.broadcast_to(values[:, None, :], (LEV, 8, count)).reshape(LEV * 8, count)


def kernel(
    c0_ref, kx_ref, ky_ref, w_ref, jac_ref, innov_ref, dest_ref, cell_ref,
    control_ref, residual_ref,
    jac, innov, innov_wide, line, table, mixed, pad_a, pad_b, send_g, recv_g, pack, send_m, recv_m,
    model, extra, onehot, autocov, near_x, place, cells, queue_a, queue_b, recv_a, recv_b,
    field, high_field, part, sums_x, sums_y, send_f, recv_f,
    load_sem, dense_send, dense_recv, model_send, model_recv, cell_send, cell_recv,
    qa_send, qa_recv, qb_send, qb_recv, sx_send, sx_recv, sy_send, sy_recv, final_send, final_recv,
):
    my_x, my_y = lax.axis_index("px"), lax.axis_index("py")
    me = my_x * NPY + my_y

    def device(index):
        return (index // NPY, index % NPY)

    load_jac = pltpu.make_async_copy(jac_ref, jac, load_sem.at[0])
    load_innov = pltpu.make_async_copy(innov_ref, innov, load_sem.at[1])
    load_jac.start()
    load_innov.start()

    barrier = pltpu.get_barrier_semaphore()

    @pl.loop(1, ND)
    def _(step):
        pl.semaphore_signal(
            barrier, inc=1, device_id=device(lax.rem(me + step, ND)), device_id_type=MESH
        )

    tap = iota((TAPS, 128), 0)
    place_at = iota((TAPS, 128), 1)
    pick_forward = (tap == ((32 - place_at) & 127)).astype(F32)
    pick_backward = (tap == ((place_at + 32) & 127)).astype(F32)
    for which, (taps_ref, pick) in enumerate(
        ((kx_ref, pick_forward), (kx_ref, pick_backward), (ky_ref, pick_forward), (ky_ref, pick_backward))
    ):
        line[which] = dot(taps_ref[...], pick, precision=HIGHEST)

    inside = jnp.abs(iota((128, 128), 0) - iota((128, 128), 1)) < 64

    def circulant(row):
        return pltpu.roll(jnp.broadcast_to(row, (128, 128)), 0, 1, stride=1, stride_axis=0)

    def build_table(which):
        @pl.loop(0, LEV)
        def _(level):
            ring = circulant(line[which, pl.ds(level, 1), :])
            both = jnp.concatenate([jnp.where(inside, ring, 0.0), jnp.where(inside, 0.0, ring)], axis=0)
            high, low = split(both)
            table[which, level] = jnp.concatenate([high, low], axis=1)

    lower_half = iota((64, 128), 1) < 64

    def convolve(own, before, after, which, level):
        count = own.shape[0]
        beside = jnp.where(iota((count, 128), 1) < 64, after, before)
        product = dot(stacked(jnp.concatenate([own, beside], axis=1)), table[which, level])
        upper, lower = product[:count], product[count:]
        return (upper[:, :128] + upper[:, 128:]) + (lower[:, :128] + lower[:, 128:])

    build_table(FX)

    @pl.loop(0, LEV)
    def _(level):
        blocks = [c0_ref[level, :, 128 * b : 128 * b + 128] for b in range(8)]
        own = jnp.concatenate(blocks, axis=0)
        before = jnp.concatenate(blocks[7:] + blocks[:7], axis=0)
        after = jnp.concatenate(blocks[1:] + blocks[:1], axis=0)
        out = convolve(own, before, after, FX, level)
        for b in range(8):
            mixed[b, level] = out[8 * b : 8 * b + 8]

    @pl.loop(0, 8)
    def _(block):
        tiles = swap_groups([mixed[block, level] for level in range(LEV)])
        for j in range(16):
            send_g[pl.ds(pl.multiple_of(128 * block + 8 * j, 8), 8), :] = tiles[j]

    pl.semaphore_wait(barrier, ND - 1)

    def exchange(source, target, rows, send_sem, recv_sem):
        mine = pl.ds(pl.multiple_of(me * rows, rows), rows)

        @pl.loop(1, ND)
        def _(step):
            other = lax.rem(me + step, ND)
            pltpu.make_async_remote_copy(
                src_ref=source.at[pl.ds(pl.multiple_of(other * rows, rows), rows)],
                dst_ref=target.at[mine],
                send_sem=send_sem,
                recv_sem=recv_sem,
                device_id=device(other),
                device_id_type=MESH,
            ).start()

        target[mine, :] = source[mine, :]
        whole = pl.ds(0, (ND - 1) * rows)
        return pltpu.make_async_remote_copy(
            src_ref=source.at[whole],
            dst_ref=target.at[whole],
            send_sem=send_sem,
            recv_sem=recv_sem,
            device_id=device(lax.rem(me + 1, ND)),
            device_id_type=MESH,
        )

    dense = exchange(send_g, recv_g, 8, dense_send, dense_recv)

    load_jac.wait()
    load_innov.wait()
    innov_wide[...] = innov[...].astype(F32)

    def one_channel(channel, carry):
        values = jac[channel].astype(F32)
        scaled = values * w_ref[channel]
        matrix, rhs = carry
        matrix = tuple(
            m + scaled * jnp.broadcast_to(values[k : k + 1], (LEV, 128)) for k, m in enumerate(matrix)
        )
        return matrix, rhs + scaled * jnp.broadcast_to(innov_wide[pl.ds(channel, 1), :], (LEV, 128))

    zero = jnp.zeros((LEV, 128), F32)
    matrix, rhs = lax.fori_loop(0, CH, one_channel, ((zero,) * LEV, zero))
    for k in range(LEV):
        pack[16 * k : 16 * k + 16, :] = matrix[k]
    pack[256:272, :] = rhs
    pack[272:384, :] = jnp.zeros((112, 128), F32)
    pack[272:273, :] = cell_ref[...].astype(F32) + 1.0

    dest = jnp.broadcast_to(dest_ref[...], (128, 128))
    dest_t = jnp.transpose(dest.astype(F32))
    earlier = (dest.astype(F32) == dest_t) & (iota((128, 128), 0) < iota((128, 128), 1))
    rank = jnp.sum(earlier.astype(F32), axis=0, keepdims=True)
    named = iota((128, 128), 0) == dest
    chosen = jnp.concatenate(
        [(named & (rank == float(k))).astype(BF16) for k in range(2)], axis=0
    )
    pack_high, pack_low = split(pack[...])
    packed = dot(chosen, pack_high, NT) + dot(chosen, pack_low, NT)
    send_m[...] = jnp.zeros_like(send_m)
    for k in range(2):
        for i in range(3):
            send_m[pl.ds(4 * k + i, 128, stride=8), :] = packed[128 * k : 128 * k + 128, 128 * i : 128 * i + 128]

    models = exchange(send_m, recv_m, 8, model_send, model_recv)

    build_table(FY)
    build_table(BY)
    build_table(BX)

    column = iota((8, 128), 1)
    offset = iota((8, 128), 0)

    @pl.loop(0, LEV)
    def _(level):
        taps = line[BX, pl.ds(level, 1), :]
        rows = jnp.broadcast_to(taps, (8, 128))
        cov = dot(rows, circulant(line[BX, pl.ds(level, 1), :]), NT, precision=HIGHEST)
        ring = pltpu.roll(cov, 64, 1, stride=1, stride_axis=0)
        at = pl.ds(pl.multiple_of(8 * level, 8), 8)
        autocov[0, at, :] = jnp.where(column > offset, ring, 0.0)
        autocov[1, at, :] = jnp.where(column < offset, ring, 0.0)

    for block in (0, 9):
        pad_a[:, 8 * block : 8 * block + 8, :] = jnp.zeros((LEV, 8, 128), F32)
        pad_b[:, 8 * block : 8 * block + 8, :] = jnp.zeros((LEV, 8, 128), F32)

    def along_rows(source, which, level):
        return convolve(
            source[level, 8:72, :], source[level, 0:64, :], source[level, 16:80, :], which, level
        )

    dense.wait_recv()

    @pl.loop(0, 8)
    def _(block):
        turned = jnp.transpose(recv_g[pl.ds(pl.multiple_of(128 * block, 128), 128), :])
        pad_a[:, pl.ds(pl.multiple_of(8 + 8 * block, 8), 8), :] = turned.reshape(LEV, 8, 128)

    def filter_to_field(source):
        @pl.loop(0, LEV)
        def _(level):
            out = along_rows(source, FY, level)
            at = pl.ds(pl.multiple_of(8 * level, 8), 8)
            for b in range(8):
                high_field[at, 128 * b : 128 * b + 128] = out[8 * b : 8 * b + 8]

    filter_to_field(pad_a)

    models.wait_recv()
    for k in range(2):
        lanes = slice(128 * k, 128 * k + 128)
        for i in range(2):
            turned = jnp.transpose(recv_m[pl.ds(4 * k + i, 128, stride=8), :])
            model[8 * i : 8 * i + 8, :, lanes] = turned.reshape(8, LEV, 128)
        turned = jnp.transpose(recv_m[pl.ds(4 * k + 2, 128, stride=8), :])
        extra[0:24, lanes] = turned[0:24]
    code = extra[16:17, :] - 1.0
    cell_x = jnp.floor(code * (1.0 / 1024.0))
    cell_y = jnp.where(code < 0.0, -1.0, code - 1024.0 * cell_x)
    cells[...] = jnp.concatenate([cell_x, cell_y, jnp.zeros((6, 256), F32)], axis=0)
    place[MIDDLE] = cells[...]

    def neighbour_copy(source, target, send_sem, recv_sem, slot):
        other = lax.rem(me - (slot - MIDDLE) + ND, ND)
        return pltpu.make_async_remote_copy(
            src_ref=source,
            dst_ref=target.at[slot],
            send_sem=send_sem.at[slot],
            recv_sem=recv_sem.at[slot],
            device_id=device(other),
            device_id_type=MESH,
        )

    def for_neighbours(action):
        @pl.loop(0, NEAR - 1)
        def _(index):
            action(index + (index >= MIDDLE).astype(I32))

    for_neighbours(lambda slot: neighbour_copy(cells, place, cell_send, cell_recv, slot).start())

    row_number = iota((128, 256), 0).astype(F32)

    def build_onehot(slot):
        row_of = place[slot, 1:2, :]

        @pl.loop(0, 8)
        def _(block):
            base = (128 * block).astype(F32)
            hit = (row_number + base) == row_of
            onehot[slot, pl.ds(pl.multiple_of(128 * block, 128), 128), :] = hit.astype(BF16)

        column_of = place[slot, 0:1, :]
        wraps = slot == NEAR - 1
        first = jnp.where(wraps, 0, 8 * slot).astype(F32)
        hit = (row_number == column_of + first).astype(BF16)
        product = dot(stacked(autocov[jnp.where(wraps, 1, 0)]), hit)
        near_x[slot] = product[:128] + product[128:]

    build_onehot(MIDDLE)
    own_column = jnp.broadcast_to(place[MIDDLE, 0:1, :], (8, 256)) == iota((8, 256), 0).astype(F32)

    def sample():
        high, low = split(high_field[...])
        product = dot(high, onehot[MIDDLE]) + dot(low, onehot[MIDDLE])
        return jnp.sum(jnp.where(own_column[None], product.reshape(LEV, 8, 256), 0.0), axis=1)

    def apply_model(values):
        total = jnp.zeros((LEV, 256), F32)
        for k in range(LEV):
            total = total + model[k] * jnp.broadcast_to(values[k : k + 1], (LEV, 256))
        return total

    z0 = sample()
    q1 = apply_model(z0) - extra[0:16, :]
    queue_a[...] = q1
    recv_a[MIDDLE] = q1
    for_neighbours(lambda slot: neighbour_copy(queue_a, recv_a, qa_send, qa_recv, slot).start())

    def arrive_cells(slot):
        neighbour_copy(cells, place, cell_send, cell_recv, slot).wait_recv()
        build_onehot(slot)

    for_neighbours(arrive_cells)

    def covary(source, target, send_sem, recv_sem):
        field[...] = jnp.zeros_like(field)

        def add(slot):
            spread = near_x[slot] * spread_levels(target[slot])
            pair = stacked(spread)

            @pl.loop(0, 4)
            def _(quarter):
                at = pl.ds(pl.multiple_of(256 * quarter, 256), 256)
                field[quarter] += dot(pair, onehot[slot, at, :], NT)

        add(MIDDLE)

        def arrived(slot):
            neighbour_copy(source, target, send_sem, recv_sem, slot).wait_recv()
            add(slot)

        for_neighbours(arrived)
        fill_pad(field)

        @pl.loop(0, LEV)
        def _(level):
            pad_b[level, 8:72, :] = along_rows(pad_a, BY, level)

        filter_to_field(pad_b)
        return sample()

    def fill_pad(source):
        @pl.loop(0, 4)
        def _(quarter):
            total = source[quarter, 0:128, :] + source[quarter, 128:256, :]
            for half in range(2):
                rows = pl.ds(pl.multiple_of(8 + 16 * quarter + 8 * half, 8), 8)
                pad_a[:, rows, :] = total[:, 128 * half : 128 * half + 128].reshape(LEV, 8, 128)

    t1 = covary(queue_a, recv_a, qa_send, qa_recv)
    s0 = -(z0 + t1)
    q2 = apply_model(s0)
    queue_b[...] = q2
    recv_b[MIDDLE] = q2
    for_neighbours(lambda slot: neighbour_copy(queue_b, recv_b, qb_send, qb_recv, slot).start())
    t2 = covary(queue_b, recv_b, qb_send, qb_recv)
    u = apply_model(t2)

    def partial(first, second):
        product = jnp.sum(first * second, axis=0, keepdims=True)
        return product[:, :128] + product[:, 128:]

    start = jnp.sum(jnp.sum((c0_ref[...] * c0_ref[...]).reshape(LEV * 8, 1024), axis=0, keepdims=True).reshape(8, 128), axis=0, keepdims=True)
    part[...] = jnp.concatenate(
        [start, partial(z0, q1), partial(q1, t1), partial(s0, q2), partial(t2, q2), partial(t2, u),
         jnp.zeros((2, 128), F32)], axis=0)

    def sum_over(source, target, count, mine, other_of, send_sem, recv_sem):
        @pl.loop(1, count)
        def _(step):
            pltpu.make_async_remote_copy(
                src_ref=source,
                dst_ref=target.at[mine],
                send_sem=send_sem,
                recv_sem=recv_sem,
                device_id=other_of(lax.rem(mine + step, count)),
                device_id_type=MESH,
            ).start()

        target[mine] = source[...]
        whole = pltpu.make_async_remote_copy(
            src_ref=target.at[pl.ds(0, count - 1)],
            dst_ref=target.at[pl.ds(0, count - 1)],
            send_sem=send_sem,
            recv_sem=recv_sem,
            device_id=other_of(lax.rem(mine + 1, count)),
            device_id_type=MESH,
        )
        whole.wait_recv()
        whole.wait_send()
        return jnp.sum(target[...], axis=0)

    part_x = sum_over(part, sums_x, NPX, my_x, lambda o: (o, my_y), sx_send, sx_recv)
    part[...] = part_x
    total = sum_over(part, sums_y, NPY, my_y, lambda o: (my_x, o), sy_send, sy_recv)
    scalar = jnp.sum(total, axis=1, keepdims=True)
    c0c0, z0q1, q1t1, s0q2, q2t2, t2u = [scalar[k : k + 1] for k in range(6)]
    norm0 = c0c0 + 2.0 * z0q1 + q1t1
    alpha0 = norm0 / (norm0 + s0q2)
    keep = 1.0 - alpha0
    norm1 = keep * keep * norm0 - 2.0 * alpha0 * keep * s0q2 + alpha0 * alpha0 * q2t2
    beta0 = norm1 / norm0
    gain = keep + beta0
    curvature = gain * gain * s0q2 - 2.0 * gain * alpha0 * q2t2 + alpha0 * alpha0 * t2u
    alpha1 = norm1 / (norm1 + beta0 * beta0 * norm0 + curvature)
    coef_c = alpha0 + alpha1 * gain
    coef_r = (1.0 - alpha1) * keep - alpha1 * beta0
    y_control = coef_c * q1 + (alpha0 * alpha1) * q2
    y_residual = coef_r * q1 + ((1.0 - alpha1) * alpha0) * q2 + alpha1 * (gain * q2 - alpha0 * u)

    own_mask = jnp.broadcast_to(own_column[None], (LEV, 8, 256)).reshape(LEV * 8, 256)

    for index, values in enumerate((y_control, y_residual)):
        pair = stacked(jnp.where(own_mask, spread_levels(values), 0.0))

        @pl.loop(0, 4)
        def _(quarter):
            at = pl.ds(pl.multiple_of(256 * quarter, 256), 256)
            field[quarter] = dot(pair, onehot[MIDDLE, at, :], NT)

        fill_pad(field)

        @pl.loop(0, LEV)
        def _(level):
            out = along_rows(pad_a, BY, level)
            for b in range(8):
                mixed[8 * index + b, level] = out[8 * b : 8 * b + 8]

    @pl.loop(0, 8)
    def _(block):
        first = swap_groups([mixed[block, level] for level in range(LEV)])
        second = swap_groups([mixed[8 + block, level] for level in range(LEV)])
        for j in range(16):
            at = pl.ds(pl.multiple_of(256 * block + 16 * j, 16), 16)
            send_f[at, :] = jnp.concatenate([first[j], second[j]], axis=0).astype(BF16)

    final = exchange(send_f, recv_f, 16, final_send, final_recv)
    final.wait_recv()

    @pl.loop(0, 8)
    def _(block):
        arrived = recv_f[pl.ds(pl.multiple_of(256 * block, 256), 256), :].astype(F32)
        arrived = arrived.reshape(16, 2, 8, 128)
        for index in range(2):
            turned = jnp.transpose(arrived[:, index].reshape(128, 128))
            mixed[8 * index + block] = turned.reshape(LEV, 8, 128)

    for index, (out_ref, coef) in enumerate(((control_ref, 1.0 - coef_c), (residual_ref, -coef_r))):
        @pl.loop(0, LEV)
        def _(level):
            blocks = [mixed[8 * index + b, level] for b in range(8)]
            own = jnp.concatenate(blocks, axis=0)
            before = jnp.concatenate(blocks[7:] + blocks[:7], axis=0)
            after = jnp.concatenate(blocks[1:] + blocks[:1], axis=0)
            out = convolve(own, before, after, BX, level)
            for b in range(8):
                lanes = slice(128 * b, 128 * b + 128)
                out_ref[level, :, lanes] = coef * c0_ref[level, :, lanes] - out[8 * b : 8 * b + 8]

    dense.wait_send()
    models.wait_send()
    final.wait_send()

    def sent(slot):
        neighbour_copy(cells, place, cell_send, cell_recv, slot).wait_send()
        neighbour_copy(queue_a, recv_a, qa_send, qa_recv, slot).wait_send()
        neighbour_copy(queue_b, recv_b, qb_send, qb_recv, slot).wait_send()

    for_neighbours(sent)


def per_device(
    control_init, kernel_x, kernel_y, obs_weight, jacobian, innovation, obs_dest, obs_cell
):
    vmem = pl.BlockSpec(memory_space=pltpu.VMEM)
    anywhere = pl.BlockSpec(memory_space=pl.ANY)
    shape = jax.ShapeDtypeStruct(control_init.shape, F32)
    dma = pltpu.SemaphoreType.DMA
    return pl.pallas_call(
        kernel,
        out_shape=(shape, shape),
        in_specs=[vmem, vmem, vmem, pl.BlockSpec(memory_space=pltpu.SMEM), anywhere, anywhere, vmem, vmem],
        out_specs=(vmem, vmem),
        scratch_shapes=[
            pltpu.VMEM((CH, LEV, 128), BF16),
            pltpu.VMEM((CH, 128), BF16),
            pltpu.VMEM((CH, 128), F32),
            pltpu.VMEM((4, LEV, 128), F32),
            pltpu.VMEM((4, LEV, 256, 256), BF16),
            pltpu.VMEM((16, LEV, 8, 128), F32),
            pltpu.VMEM((LEV, 80, 128), F32),
            pltpu.VMEM((LEV, 80, 128), F32),
            pltpu.VMEM((1024, 128), F32),
            pltpu.VMEM((1024, 128), F32),
            pltpu.VMEM((384, 128), F32),
            pltpu.VMEM((1024, 128), F32),
            pltpu.VMEM((1024, 128), F32),
            pltpu.VMEM((LEV, LEV, 256), F32),
            pltpu.VMEM((24, 256), F32),
            pltpu.VMEM((NEAR, 1024, 256), BF16),
            pltpu.VMEM((2, 128, 128), F32),
            pltpu.VMEM((NEAR, 128, 256), F32),
            pltpu.VMEM((NEAR, 8, 256), F32),
            pltpu.VMEM((8, 256), F32),
            pltpu.VMEM((LEV, 256), F32),
            pltpu.VMEM((LEV, 256), F32),
            pltpu.VMEM((NEAR, LEV, 256), F32),
            pltpu.VMEM((NEAR, LEV, 256), F32),
            pltpu.VMEM((4, 256, 256), F32),
            pltpu.VMEM((128, 1024), F32),
            pltpu.VMEM((8, 128), F32),
            pltpu.VMEM((NPX, 8, 128), F32),
            pltpu.VMEM((NPY, 8, 128), F32),
            pltpu.VMEM((2048, 128), BF16),
            pltpu.VMEM((2048, 128), BF16),
            dma((2,)),
            dma, dma, dma, dma,
            dma((NEAR,)), dma((NEAR,)),
            dma((NEAR,)), dma((NEAR,)), dma((NEAR,)), dma((NEAR,)),
            dma, dma, dma, dma, dma, dma,
        ],
        compiler_params=pltpu.CompilerParams(
            collective_id=0, has_side_effects=True, vmem_limit_bytes=52 * 1024 * 1024
        ),
    )(
        control_init,
        kernel_x,
        kernel_y,
        obs_weight,
        jnp.transpose(jacobian, (2, 1, 0)),
        jnp.transpose(innovation),
        jnp.transpose(obs_dest),
        obs_cell.reshape(1, -1),
    )


def solution(mesh):
    in_specs = (
        P(None, ("px", "py"), None),
        P(),
        P(),
        P(),
        P(("px", "py"), None, None),
        P(("px", "py"), None),
        P(("px", "py"), None),
        P(("px", "py")),
    )
    out_specs = (P(None, ("px", "py"), None), P(None, ("px", "py"), None))
    return jax.shard_map(
        per_device, mesh=mesh, in_specs=in_specs, out_specs=out_specs, check_vma=False
    )
```

```python
import functools

import jax
import jax.numpy as jnp
from jax import lax
from jax.experimental import pallas as pl
from jax.experimental.pallas import tpu as pltpu
from jax.sharding import PartitionSpec as P

F32, BF16, I32 = jnp.float32, jnp.bfloat16, jnp.int32
MESH = pl.DeviceIdType.MESH
ND, NPX, NPY = 128, 8, 16
LEV, CH, TAPS = 16, 431, 64
NEAR = 17
MIDDLE = 8
REACH = NEAR * 256
FX, BX, FY, BY = range(4)
NT = (((1,), (1,)), ((), ()))
NN = (((1,), (0,)), ((), ()))
HIGHEST = lax.Precision.HIGHEST


def iota(shape, axis):
    return lax.broadcasted_iota(I32, shape, axis)


def split(values):
    high = values.astype(BF16)
    low = (values - high.astype(F32)).astype(BF16)
    return high, low


def stacked(values):
    return jnp.concatenate(split(values), axis=0)


def dot(left, right, dims=NN, precision=None):
    return lax.dot_general(left, right, dims, precision=precision, preferred_element_type=F32)


def swap_groups(tiles):
    group = iota((8, 128), 1) // 8
    tiles = list(tiles)
    for bit in range(4):
        step = 1 << bit
        upper = (group & step) != 0
        for a in range(16):
            if a & step == 0:
                first, second = tiles[a], tiles[a + step]
                tiles[a] = jnp.where(upper, pltpu.roll(second, 8 * step, 1), first)
                tiles[a + step] = jnp.where(upper, second, pltpu.roll(first, 128 - 8 * step, 1))
    return tiles


def spread_levels(values):
    count = values.shape[1]
    return jnp.broadcast_to(values[:, None, :], (LEV, 8, count)).reshape(LEV * 8, count)


def kernel(
    c0_hbm, kx_hbm, ky_hbm, w_hbm, jac_hbm, innov_hbm, dest_hbm, cell_hbm,
    control_ref, residual_ref,
    c0_ref, kx_ref, ky_ref, w_ref, jac, innov, dest_ref, cell_ref,
    innov_wide, line, table, mixed, tile_m, send_g, recv_g, wide,
    model, extra, onehot, onehot_rows, autocov, near_x, place, cells, queue_a, queue_b,
    recv_a, recv_b, spread_q, grid, high_field, adjoint, part, sums, send_f, recv_f,
    load_sem, dense_send, dense_recv, cell_send, cell_recv,
    qa_send, qa_recv, qb_send, qb_recv, sum_send, sum_recv, final_send, final_recv,
):
    my_x, my_y = lax.axis_index("px"), lax.axis_index("py")
    me = my_x * NPY + my_y

    def device(index):
        return (index >> 4, index & 15)

    loads = [
        pltpu.make_async_copy(source, target, load_sem.at[i])
        for i, (source, target) in enumerate(
            (
                (c0_hbm, c0_ref), (kx_hbm, kx_ref), (ky_hbm, ky_ref), (w_hbm, w_ref),
                (jac_hbm, jac), (innov_hbm, innov), (dest_hbm, dest_ref), (cell_hbm, cell_ref),
            )
        )
    ]
    for load in loads:
        load.start()

    barrier = pltpu.get_barrier_semaphore()

    @pl.loop(1, ND)
    def _(step):
        pl.semaphore_signal(
            barrier, inc=1, device_id=device((me + step) & (ND - 1)), device_id_type=MESH
        )

    loads[1].wait()
    loads[2].wait()
    tap = iota((TAPS, 128), 0)
    place_at = iota((TAPS, 128), 1)
    pick_forward = (tap == ((32 - place_at) & 127)).astype(F32)
    pick_backward = (tap == ((place_at + 32) & 127)).astype(F32)
    for which, (taps_ref, pick) in enumerate(
        ((kx_ref, pick_forward), (kx_ref, pick_backward), (ky_ref, pick_forward), (ky_ref, pick_backward))
    ):
        line[which] = dot(taps_ref[...], pick, precision=HIGHEST)

    inside = jnp.abs(iota((128, 128), 0) - iota((128, 128), 1)) < 64

    def circulant(row):
        return pltpu.roll(jnp.broadcast_to(row, (128, 128)), 0, 1, stride=1, stride_axis=0)

    def build_table(which):
        @pl.loop(0, LEV, unroll=4)
        def _(level):
            ring = circulant(line[which, pl.ds(level, 1), :])
            high, low = split(ring)
            pair = jnp.concatenate([high, low], axis=1)
            nil = jnp.zeros((), BF16)
            keep = jnp.concatenate([inside, inside], axis=1)
            table[which, level, 0:128, :] = jnp.where(keep, pair, nil)
            table[which, level, 128:256, :] = jnp.where(keep, nil, pair)

    def convolve(own, before, after, which, level):
        count = own.shape[0]
        beside = jnp.where(iota((count, 128), 1) < 64, after, before)
        product = dot(stacked(jnp.concatenate([own, beside], axis=1)), table[which, level])
        upper, lower = product[:count], product[count:]
        return (upper[:, :128] + upper[:, 128:]) + (lower[:, :128] + lower[:, 128:])

    def along_x(own, which, level):
        before = jnp.concatenate([own[56:], own[:56]], axis=0)
        after = jnp.concatenate([own[8:], own[:8]], axis=0)
        return convolve(own, before, after, which, level)

    edge = jnp.zeros((8, 128), F32)

    def along_y(own, which, level):
        before = jnp.concatenate([edge, own[:56]], axis=0)
        after = jnp.concatenate([own[8:], edge], axis=0)
        return convolve(own, before, after, which, level)

    build_table(FX)
    loads[0].wait()

    for level in range(LEV):
        own = jnp.concatenate([c0_ref[level, :, 128 * b : 128 * b + 128] for b in range(8)], axis=0)
        out = along_x(own, FX, level)
        for b in range(8):
            mixed[b, level] = out[8 * b : 8 * b + 8]

    for load in loads[3:]:
        load.wait()
    innov_wide[...] = innov[...].astype(F32)

    def one_channel(channel, carry):
        values = jac[channel].astype(F32)
        scaled = values * w_ref[channel]
        matrix, rhs = carry
        matrix = tuple(
            m + scaled * jnp.broadcast_to(values[k : k + 1], (LEV, 128)) for k, m in enumerate(matrix)
        )
        return matrix, rhs + scaled * jnp.broadcast_to(innov_wide[pl.ds(channel, 1), :], (LEV, 128))

    def some_channels(index, carry):
        for k in range(8):
            carry = one_channel(8 * index + k, carry)
        return carry

    zero = jnp.zeros((LEV, 128), F32)
    carry = lax.fori_loop(0, CH // 8, some_channels, ((zero,) * LEV, zero))
    for channel in range(CH // 8 * 8, CH):
        carry = one_channel(channel, carry)
    matrix, rhs = carry

    cell = cell_ref[...]
    rhs_high, rhs_low = split(rhs)
    codes = jnp.concatenate([(cell >> 10) + 1, (cell & 1023) >> 3, cell & 7, jnp.zeros((93, 128), I32)], axis=0)
    pack = jnp.concatenate(
        [m.astype(BF16) for m in matrix] + [rhs_high, rhs_low, codes.astype(F32).astype(BF16)], axis=0
    )
    dest = jnp.broadcast_to(dest_ref[...], (128, 128))
    dest_t = jnp.transpose(dest.astype(F32))
    earlier = (dest.astype(F32) == dest_t) & (iota((128, 128), 0) < iota((128, 128), 1))
    rank = jnp.sum(earlier.astype(F32), axis=0, keepdims=True)
    named = iota((128, 128), 0) == dest
    chosen = jnp.concatenate([(named & (rank == float(k))).astype(BF16) for k in range(2)], axis=0)
    packed = dot(chosen, pack, NT)
    for k in range(2):
        for i in range(3):
            tile_m[pl.ds(3 * k + i, 128, stride=8), :] = packed[128 * k : 128 * k + 128, 128 * i : 128 * i + 128]
    for i in range(6, 8):
        tile_m[pl.ds(i, 128, stride=8), :] = jnp.zeros((128, 128), F32)

    @pl.loop(0, 8)
    def _(block):
        tiles = swap_groups([mixed[block, level] for level in range(LEV)])
        for j in range(16):
            lower = tile_m[pl.ds(pl.multiple_of(128 * block + 8 * j, 8), 8), :]
            at = pl.ds(pl.multiple_of(256 * block + 16 * j, 16), 16)
            send_g[at, :] = jnp.concatenate([tiles[j], lower], axis=0).astype(BF16)

    pl.semaphore_wait(barrier, ND - 1)

    def exchange(source, target, rows, source_of, send_sem, recv_sem):
        mine = pl.ds(pl.multiple_of(me * rows, rows), rows)

        @pl.loop(1, ND)
        def _(step):
            other = (me + step) & (ND - 1)
            pltpu.make_async_remote_copy(
                src_ref=source.at[source_of(other)],
                dst_ref=target.at[mine],
                send_sem=send_sem,
                recv_sem=recv_sem,
                device_id=device(other),
                device_id_type=MESH,
            ).start()

        target[mine, :] = source[source_of(me), :]
        whole = pl.ds(0, (ND - 1) * rows)
        return pltpu.make_async_remote_copy(
            src_ref=target.at[whole],
            dst_ref=target.at[whole],
            send_sem=send_sem,
            recv_sem=recv_sem,
            device_id=device((me + 1) & (ND - 1)),
            device_id_type=MESH,
        )

    def tile_of(index):
        return pl.ds(pl.multiple_of(index * 16, 16), 16)

    dense = exchange(send_g, recv_g, 16, tile_of, dense_send, dense_recv)

    build_table(FY)
    build_table(BY)
    build_table(BX)

    column = iota((8, 128), 1)
    offset = iota((8, 128), 0)

    @pl.loop(0, LEV, unroll=4)
    def _(level):
        taps = line[BX, pl.ds(level, 1), :]
        cov = dot(jnp.broadcast_to(taps, (8, 128)), circulant(taps), NT, precision=HIGHEST)
        ring = pltpu.roll(cov, 64, 1, stride=1, stride_axis=0)
        at = pl.ds(pl.multiple_of(8 * level, 8), 8)
        autocov[0, at, :] = jnp.where(column > offset, ring, 0.0)
        autocov[1, at, :] = jnp.where(column < offset, ring, 0.0)

    dense.wait_recv()

    for block in range(8):
        values = recv_g[256 * block : 256 * block + 256, :].astype(F32)
        wide[256 * block : 256 * block + 256, :] = values
        turned = jnp.transpose(values.reshape(16, 16, 128)[:, 0:8].reshape(128, 128))
        grid[:, 8 * block : 8 * block + 8, :] = turned.reshape(LEV, 8, 128)

    for k in range(2):
        lanes = slice(128 * k, 128 * k + 128)
        for i in range(2):
            turned = jnp.transpose(wide[pl.ds(8 + 3 * k + i, 128, stride=16), :])
            model[8 * i : 8 * i + 8, :, lanes] = turned.reshape(8, LEV, 128)
        turned = jnp.transpose(wide[pl.ds(8 + 3 * k + 2, 128, stride=16), :])
        extra[:, lanes] = turned[0:40]
        cell_x = turned[32:33] - 1.0
        cell_y = jnp.where(cell_x < 0.0, -1.0, 8.0 * turned[33:34] + turned[34:35])
        cells[k : k + 1, :] = cell_x
        cells[2 + k : 3 + k, :] = cell_y
    cells[4:8, :] = jnp.zeros((4, 128), F32)
    place[MIDDLE] = cells[...]

    def neighbour_copy(source, target, send_sem, recv_sem, slot):
        other = (me - (slot - MIDDLE)) & (ND - 1)
        return pltpu.make_async_remote_copy(
            src_ref=source,
            dst_ref=target.at[slot],
            send_sem=send_sem.at[slot],
            recv_sem=recv_sem.at[slot],
            device_id=device(other),
            device_id_type=MESH,
        )

    def for_neighbours(action, unroll=1):
        @pl.loop(0, NEAR - 1, unroll=unroll)
        def _(index):
            action(index + (index >= MIDDLE).astype(I32))

    for_neighbours(lambda slot: neighbour_copy(cells, place, cell_send, cell_recv, slot).start())

    def filter_to_field(level, own):
        out = along_y(own, FY, level)
        for b in range(8):
            high_field[8 * level : 8 * level + 8, 128 * b : 128 * b + 128] = out[8 * b : 8 * b + 8]

    for level in range(LEV):
        filter_to_field(level, grid[level])

    def both(slot, row):
        return jnp.concatenate([place[slot, row : row + 1, :], place[slot, row + 1 : row + 2, :]], axis=1)

    own_rows = both(MIDDLE, 2)
    row_number = iota((128, 256), 0).astype(F32)
    for block in range(8):
        hit = (row_number + float(128 * block)) == own_rows
        onehot_rows[128 * block : 128 * block + 128, :] = hit.astype(BF16)
    own_columns = both(MIDDLE, 0)
    own_column = jnp.broadcast_to(own_columns, (8, 256)) == iota((8, 256), 0).astype(F32)
    own_mask = jnp.broadcast_to(own_column[None], (LEV, 8, 256)).reshape(LEV * 8, 256)

    def sample():
        product = dot(stacked(high_field[...]), onehot_rows[...])
        product = product[:128] + product[128:]
        return jnp.sum(jnp.where(own_column[None], product.reshape(LEV, 8, 256), 0.0), axis=1)

    def apply_model(values):
        total = jnp.zeros((LEV, 256), F32)
        for k in range(LEV):
            total = total + model[k] * jnp.broadcast_to(values[k : k + 1], (LEV, 256))
        return total

    z0 = sample()
    q1 = apply_model(z0) - (extra[0:16, :] + extra[16:32, :])
    queue_a[...] = q1
    recv_a[MIDDLE] = q1
    for_neighbours(lambda slot: neighbour_copy(queue_a, recv_a, qa_send, qa_recv, slot).start())

    lane_number = iota((256, 128), 1).astype(F32)

    def build_onehot(slot):
        base = 256 * slot if isinstance(slot, int) else pl.multiple_of(256 * slot, 256)
        rows = place[slot]
        turned = jnp.transpose(jnp.concatenate([rows] + [jnp.zeros((8, 128), F32)] * 15, axis=0))
        rows_of = jnp.concatenate([turned[:, 2:3], turned[:, 3:4]], axis=0)
        rows_of = jnp.broadcast_to(rows_of, (256, 128))
        for block in range(8):
            hit = (lane_number + float(128 * block)) == rows_of
            onehot[pl.ds(base, 256), 128 * block : 128 * block + 128] = hit.astype(BF16)

        columns_of = both(slot, 0)
        wraps = slot == NEAR - 1
        first = jnp.where(wraps, 0, 8 * slot).astype(F32)
        hit = (row_number == columns_of + first).astype(BF16)
        product = dot(stacked(autocov[jnp.where(wraps, 1, 0)]), hit)
        near_x[slot] = product[:128] + product[128:]

    build_onehot(MIDDLE)

    def to_grid(pair, first, count, then):
        for quarter in range(4):
            total = dot(pair, onehot[first : first + count, 256 * quarter : 256 * quarter + 256])
            total = total[0:128] + total[128:256]
            for half in range(2):
                at = 16 * quarter + 8 * half
                grid[:, at : at + 8, :] = total[:, 128 * half : 128 * half + 128].reshape(LEV, 8, 128)
        for level in range(LEV):
            then(level, along_y(grid[level], BY, level))

    def own_adjoint(index, values):
        def keep(level, out):
            adjoint[index, level] = out

        to_grid(stacked(jnp.where(own_mask, spread_levels(values), 0.0)), 256 * MIDDLE, 256, keep)

    own_adjoint(0, q1)

    def arrive_cells(slot):
        neighbour_copy(cells, place, cell_send, cell_recv, slot).wait_recv()
        build_onehot(slot)

    for_neighbours(arrive_cells)

    def covary(source, target, send_sem, recv_sem):
        def add(slot):
            lanes = pl.ds(pl.multiple_of(256 * slot, 256), 256)
            spread_q[:, lanes] = stacked(near_x[slot] * spread_levels(target[slot]))

        add(MIDDLE)

        def arrived(slot):
            neighbour_copy(source, target, send_sem, recv_sem, slot).wait_recv()
            add(slot)

        for_neighbours(arrived)
        to_grid(spread_q[...], 0, REACH, filter_to_field)
        return sample()

    t1 = covary(queue_a, recv_a, qa_send, qa_recv)
    s0 = -(z0 + t1)
    q2 = apply_model(s0)
    queue_b[...] = q2
    recv_b[MIDDLE] = q2
    for_neighbours(lambda slot: neighbour_copy(queue_b, recv_b, qb_send, qb_recv, slot).start())
    own_adjoint(1, q2)
    c0c0 = jnp.sum(jnp.sum(c0_ref[...] * c0_ref[...], axis=0))
    t2 = covary(queue_b, recv_b, qb_send, qb_recv)
    u = apply_model(t2)

    lane = iota((1, 128), 1)
    row = jnp.zeros((1, 128), F32)
    for k, value in enumerate(
        (c0c0, jnp.sum(z0 * q1), jnp.sum(q1 * t1), jnp.sum(s0 * q2), jnp.sum(t2 * q2), jnp.sum(t2 * u))
    ):
        row = jnp.where(lane == k, value, row)
    part[...] = row
    total = exchange(part, sums, 1, lambda index: pl.ds(0, 1), sum_send, sum_recv)
    own_adjoint(2, u)
    total.wait_recv()
    summed = jnp.sum(sums[...], axis=0, keepdims=True)
    c0c0, z0q1, q1t1, s0q2, q2t2, t2u = [summed[:, k : k + 1] for k in range(6)]
    norm0 = c0c0 + 2.0 * z0q1 + q1t1
    alpha0 = norm0 / (norm0 + s0q2)
    keep = 1.0 - alpha0
    norm1 = keep * keep * norm0 - 2.0 * alpha0 * keep * s0q2 + alpha0 * alpha0 * q2t2
    beta0 = norm1 / norm0
    gain = keep + beta0
    curvature = gain * gain * s0q2 - 2.0 * gain * alpha0 * q2t2 + alpha0 * alpha0 * t2u
    alpha1 = norm1 / (norm1 + beta0 * beta0 * norm0 + curvature)
    coef_c = alpha0 + alpha1 * gain
    coef_r = (1.0 - alpha1) * keep - alpha1 * beta0
    control_2 = alpha0 * alpha1
    residual_2 = (1.0 - alpha1) * alpha0 + alpha1 * gain
    residual_u = -alpha1 * alpha0

    @pl.loop(0, 8)
    def _(block):
        at = pl.ds(pl.multiple_of(8 * block, 8), 8)
        first, second = [], []
        for level in range(LEV):
            one, two, three = [adjoint[k, level, at, :] for k in range(3)]
            first.append(coef_c * one + control_2 * two)
            second.append(coef_r * one + residual_2 * two + residual_u * three)
        first, second = swap_groups(first), swap_groups(second)
        for j in range(16):
            at = pl.ds(pl.multiple_of(256 * block + 16 * j, 16), 16)
            send_f[at, :] = jnp.concatenate([first[j], second[j]], axis=0).astype(BF16)

    final = exchange(send_f, recv_f, 16, tile_of, final_send, final_recv)
    final.wait_recv()

    for block in range(8):
        arrived = recv_f[256 * block : 256 * block + 256, :].astype(F32).reshape(16, 2, 8, 128)
        for index in range(2):
            turned = jnp.transpose(arrived[:, index].reshape(128, 128))
            adjoint[index, :, 8 * block : 8 * block + 8, :] = turned.reshape(LEV, 8, 128)

    for level in range(LEV):
        for index, (out_ref, coef) in enumerate(((control_ref, 1.0 - coef_c), (residual_ref, -coef_r))):
            out = along_x(adjoint[index, level], BX, level)
            for b in range(8):
                lanes = slice(128 * b, 128 * b + 128)
                out_ref[level, :, lanes] = coef * c0_ref[level, :, lanes] - out[8 * b : 8 * b + 8]

    dense.wait_send()
    total.wait_send()
    final.wait_send()

    def sent(slot):
        neighbour_copy(cells, place, cell_send, cell_recv, slot).wait_send()
        neighbour_copy(queue_a, recv_a, qa_send, qa_recv, slot).wait_send()
        neighbour_copy(queue_b, recv_b, qb_send, qb_recv, slot).wait_send()

    for_neighbours(sent)


def per_device(
    control_init, kernel_x, kernel_y, obs_weight, jacobian, innovation, obs_dest, obs_cell
):
    vmem = pl.BlockSpec(memory_space=pltpu.VMEM)
    anywhere = pl.BlockSpec(memory_space=pl.ANY)
    shape = jax.ShapeDtypeStruct(control_init.shape, F32)
    dma = pltpu.SemaphoreType.DMA
    return pl.pallas_call(
        kernel,
        out_shape=(shape, shape),
        in_specs=[anywhere] * 8,
        out_specs=(vmem, vmem),
        scratch_shapes=[
            pltpu.VMEM((LEV, 8, 1024), F32),
            pltpu.VMEM((LEV, TAPS), F32),
            pltpu.VMEM((LEV, TAPS), F32),
            pltpu.SMEM((CH,), F32),
            pltpu.VMEM((CH, LEV, 128), BF16),
            pltpu.VMEM((CH, 128), BF16),
            pltpu.VMEM((1, 128), I32),
            pltpu.VMEM((1, 128), I32),
            pltpu.VMEM((CH, 128), F32),
            pltpu.VMEM((4, LEV, 128), F32),
            pltpu.VMEM((4, LEV, 256, 256), BF16),
            pltpu.VMEM((8, LEV, 8, 128), F32),
            pltpu.VMEM((1024, 128), F32),
            pltpu.VMEM((2048, 128), BF16),
            pltpu.VMEM((2048, 128), BF16),
            pltpu.VMEM((2048, 128), F32),
            pltpu.VMEM((LEV, LEV, 256), F32),
            pltpu.VMEM((40, 256), F32),
            pltpu.VMEM((REACH, 1024), BF16),
            pltpu.VMEM((1024, 256), BF16),
            pltpu.VMEM((2, 128, 128), F32),
            pltpu.VMEM((NEAR, 128, 256), F32),
            pltpu.VMEM((NEAR, 8, 128), F32),
            pltpu.VMEM((8, 128), F32),
            pltpu.VMEM((LEV, 256), F32),
            pltpu.VMEM((LEV, 256), F32),
            pltpu.VMEM((NEAR, LEV, 256), F32),
            pltpu.VMEM((NEAR, LEV, 256), F32),
            pltpu.VMEM((256, REACH), BF16),
            pltpu.VMEM((LEV, 64, 128), F32),
            pltpu.VMEM((128, 1024), F32),
            pltpu.VMEM((3, LEV, 64, 128), F32),
            pltpu.VMEM((1, 128), F32),
            pltpu.VMEM((ND, 128), F32),
            pltpu.VMEM((2048, 128), BF16),
            pltpu.VMEM((2048, 128), BF16),
            dma((8,)),
            dma, dma,
            dma((NEAR,)), dma((NEAR,)),
            dma((NEAR,)), dma((NEAR,)), dma((NEAR,)), dma((NEAR,)),
            dma, dma, dma, dma,
        ],
        compiler_params=pltpu.CompilerParams(
            collective_id=0, has_side_effects=True, vmem_limit_bytes=60 * 1024 * 1024
        ),
    )(
        control_init,
        kernel_x,
        kernel_y,
        obs_weight,
        jnp.transpose(jacobian, (2, 1, 0)),
        jnp.transpose(innovation),
        jnp.transpose(obs_dest),
        obs_cell.reshape(1, -1),
    )


def solution(mesh):
    in_specs = (
        P(None, ("px", "py"), None),
        P(),
        P(),
        P(),
        P(("px", "py"), None, None),
        P(("px", "py"), None),
        P(("px", "py"), None),
        P(("px", "py")),
    )
    out_specs = (P(None, ("px", "py"), None), P(None, ("px", "py"), None))
    return jax.shard_map(
        per_device, mesh=mesh, in_specs=in_specs, out_specs=out_specs, check_vma=False
    )
```

```python
import functools

import jax
import jax.numpy as jnp
from jax import lax
from jax.experimental import pallas as pl
from jax.experimental.pallas import tpu as pltpu
from jax.sharding import PartitionSpec as P

F32, BF16, I32 = jnp.float32, jnp.bfloat16, jnp.int32
MESH = pl.DeviceIdType.MESH
ND, NPX, NPY = 128, 8, 16
LEV, CH, TAPS = 16, 431, 64
NEAR = 17
MIDDLE = 8
REACH = NEAR * 256
FX, BX, FY, BY = range(4)
NT = (((1,), (1,)), ((), ()))
NN = (((1,), (0,)), ((), ()))
HIGHEST = lax.Precision.HIGHEST


def iota(shape, axis):
    return lax.broadcasted_iota(I32, shape, axis)


def split(values):
    high = values.astype(BF16)
    low = (values - high.astype(F32)).astype(BF16)
    return high, low


def stacked(values):
    return jnp.concatenate(split(values), axis=0)


def dot(left, right, dims=NN, precision=None):
    return lax.dot_general(left, right, dims, precision=precision, preferred_element_type=F32)


def swap_groups(tiles):
    group = iota((8, 128), 1) // 8
    tiles = list(tiles)
    for bit in range(4):
        step = 1 << bit
        upper = (group & step) != 0
        for a in range(16):
            if a & step == 0:
                first, second = tiles[a], tiles[a + step]
                tiles[a] = jnp.where(upper, pltpu.roll(second, 8 * step, 1), first)
                tiles[a + step] = jnp.where(upper, second, pltpu.roll(first, 128 - 8 * step, 1))
    return tiles


def spread_levels(values):
    count = values.shape[1]
    return jnp.broadcast_to(values[:, None, :], (LEV, 8, count)).reshape(LEV * 8, count)


def kernel(
    c0_hbm, kx_hbm, ky_hbm, w_hbm, jac_hbm, innov_hbm, dest_hbm, cell_hbm,
    control_ref, residual_ref,
    c0_ref, kx_ref, ky_ref, w_ref, jac, innov, dest_ref, cell_ref,
    innov_wide, line, table, mixed, tile_m, send_g, recv_g, wide, send_m, recv_m,
    model_low, model_high, extra, onehot, onehot_rows, autocov, near_x, place, cells, queue_a, queue_b,
    recv_a, recv_b, spread_q, grid, high_field, adjoint, field, send_u, recv_u, send_f, recv_f,
    entered, load_sem, model_send, model_recv, dense_send, dense_recv, cell_send, cell_recv,
    qa_send, qa_recv, qb_send, qb_recv, early_send, early_recv, final_send, final_recv,
):
    my_x, my_y = lax.axis_index("px"), lax.axis_index("py")
    me = my_x * NPY + my_y

    def device(index):
        return (index >> 4, index & 15)

    loads = [
        pltpu.make_async_copy(source, target, load_sem.at[i])
        for i, (source, target) in enumerate(
            (
                (c0_hbm, c0_ref), (kx_hbm, kx_ref), (ky_hbm, ky_ref), (w_hbm, w_ref),
                (jac_hbm, jac), (innov_hbm, innov), (dest_hbm, dest_ref), (cell_hbm, cell_ref),
            )
        )
    ]
    for load in loads:
        load.start()

    barrier = pltpu.get_barrier_semaphore()

    for step in range(1, NPY):
        pl.semaphore_signal(
            barrier, inc=1, device_id=(my_x, (my_y + step) & (NPY - 1)), device_id_type=MESH
        )
    for step in range(1, NPX):
        pl.semaphore_signal(
            barrier, inc=1, device_id=((my_x + step) & (NPX - 1), my_y), device_id_type=MESH
        )

    loads[1].wait()
    loads[2].wait()
    tap = iota((TAPS, 128), 0)
    place_at = iota((TAPS, 128), 1)
    pick_forward = (tap == ((32 - place_at) & 127)).astype(F32)
    pick_backward = (tap == ((place_at + 32) & 127)).astype(F32)
    for which, (taps_ref, pick) in enumerate(
        ((kx_ref, pick_forward), (kx_ref, pick_backward), (ky_ref, pick_forward), (ky_ref, pick_backward))
    ):
        line[which] = dot(taps_ref[...], pick, precision=HIGHEST)

    inside = jnp.abs(iota((128, 128), 0) - iota((128, 128), 1)) < 64

    def circulant(row):
        return pltpu.roll(jnp.broadcast_to(row, (128, 128)), 0, 1, stride=1, stride_axis=0)

    def build_table(which):
        @pl.loop(0, LEV, unroll=4)
        def _(level):
            ring = circulant(line[which, pl.ds(level, 1), :])
            high, low = split(ring)
            pair = jnp.concatenate([high, low], axis=1)
            nil = jnp.zeros((), BF16)
            keep = jnp.concatenate([inside, inside], axis=1)
            table[which, level, 0:128, :] = jnp.where(keep, pair, nil)
            table[which, level, 128:256, :] = jnp.where(keep, nil, pair)

    def convolve(own, before, after, which, level):
        count = own.shape[0]
        beside = jnp.where(iota((count, 128), 1) < 64, after, before)
        product = dot(stacked(jnp.concatenate([own, beside], axis=1)), table[which, level])
        upper, lower = product[:count], product[count:]
        return (upper[:, :128] + upper[:, 128:]) + (lower[:, :128] + lower[:, 128:])

    def along_x(own, which, level):
        before = jnp.concatenate([own[56:], own[:56]], axis=0)
        after = jnp.concatenate([own[8:], own[:8]], axis=0)
        return convolve(own, before, after, which, level)

    edge = jnp.zeros((8, 128), F32)

    def along_y(own, which, level):
        before = jnp.concatenate([edge, own[:56]], axis=0)
        after = jnp.concatenate([own[8:], edge], axis=0)
        return convolve(own, before, after, which, level)

    build_table(FX)
    loads[0].wait()

    for level in range(LEV):
        own = jnp.concatenate([c0_ref[level, :, 128 * b : 128 * b + 128] for b in range(8)], axis=0)
        out = along_x(own, FX, level)
        for b in range(8):
            mixed[b, level] = out[8 * b : 8 * b + 8]

    loads[6].wait()
    loads[7].wait()
    cell = cell_ref[...]
    codes = jnp.concatenate([(cell >> 10) + 1, (cell & 1023) >> 3, cell & 7, jnp.zeros((125, 128), I32)], axis=0)
    dest = jnp.broadcast_to(dest_ref[...], (128, 128))
    dest_t = jnp.transpose(dest.astype(F32))
    earlier = (dest.astype(F32) == dest_t) & (iota((128, 128), 0) < iota((128, 128), 1))
    rank = jnp.sum(earlier.astype(F32), axis=0, keepdims=True)
    named = iota((128, 128), 0) == dest
    chosen = jnp.concatenate([(named & (rank == float(k))).astype(BF16) for k in range(2)], axis=0)
    packed = dot(chosen, codes.astype(F32).astype(BF16), NT)
    for k in range(2):
        tile_m[pl.ds(k, 128, stride=8), :] = packed[128 * k : 128 * k + 128]
    for i in range(2, 8):
        tile_m[pl.ds(i, 128, stride=8), :] = jnp.zeros((128, 128), F32)

    pl.semaphore_wait(barrier, NPX + NPY - 2)
    for step in range(1, NPX):
        pl.semaphore_signal(
            entered, inc=1, device_id=((my_x + step) & (NPX - 1), my_y), device_id_type=MESH
        )
    def send_one(source, target, rows, other, source_rows, send_sem, recv_sem):
        pltpu.make_async_remote_copy(
            src_ref=source.at[source_rows],
            dst_ref=target.at[rows],
            send_sem=send_sem,
            recv_sem=recv_sem,
            device_id=device(other),
            device_id_type=MESH,
        ).start()

    def all_sent(target, rows, send_sem, recv_sem):
        whole = pl.ds(0, (ND - 1) * rows)
        return pltpu.make_async_remote_copy(
            src_ref=target.at[whole],
            dst_ref=target.at[whole],
            send_sem=send_sem,
            recv_sem=recv_sem,
            device_id=device((me + 1) & (ND - 1)),
            device_id_type=MESH,
        )

    def rows_of(index, stride, count):
        return pl.ds(pl.multiple_of(index * stride, stride), count)

    def exchange(source, target, stride, count, send_sem, recv_sem):
        mine = rows_of(me, stride, count)

        @pl.loop(1, ND)
        def _(step):
            other = (me + step) & (ND - 1)
            send_one(source, target, mine, other, rows_of(other, stride, count), send_sem, recv_sem)

        target[mine, :] = source[mine, :]
        return all_sent(target, count, send_sem, recv_sem)

    def store_tiles(tiles, source, turn):
        block = (my_x + turn) & (NPX - 1)
        for j, tile in enumerate(tiles(block)):
            source[pl.ds(pl.multiple_of(256 * block + 16 * j, 16), 16), :] = tile.astype(BF16)

    def send_tiles(source, target, rows, turn, send_sem, recv_sem):
        mine = rows_of(me, 16, rows)
        block = (my_x + turn) & (NPX - 1)
        for j in range(1 if turn == 0 else 0, NPY):
            other = block * NPY + ((my_y + j) & (NPY - 1))
            send_one(source, target, mine, other, rows_of(other, 16, rows), send_sem, recv_sem)

    def keep_own(source, target, rows):
        mine = rows_of(me, 16, rows)
        target[mine, :] = source[mine, :]

    def first_tiles(block):
        tiles = swap_groups([mixed[block, level] for level in range(LEV)])
        lower = [tile_m[pl.ds(pl.multiple_of(128 * block + 8 * j, 8), 8), :] for j in range(16)]
        return [jnp.concatenate([tiles[j], lower[j]], axis=0) for j in range(16)]

    for turn in range(NPX):
        store_tiles(first_tiles, send_g, turn)
    send_tiles(send_g, recv_g, 16, 0, dense_send, dense_recv)
    pl.semaphore_wait(entered, NPX - 1)
    for turn in range(1, NPX):
        send_tiles(send_g, recv_g, 16, turn, dense_send, dense_recv)
    keep_own(send_g, recv_g, 16)
    dense = all_sent(recv_g, 16, dense_send, dense_recv)

    for load in loads[3:6]:
        load.wait()
    innov_wide[...] = innov[...].astype(F32)

    def one_channel(channel, carry):
        values = jac[channel].astype(F32)
        scaled = values * w_ref[channel]
        low, high, rhs = carry
        rows = [jnp.broadcast_to(values[k : k + 1], (8, 128)) for k in range(LEV)]
        low = tuple(m + scaled[0:8] * rows[k] for k, m in enumerate(low))
        high = tuple(m + scaled[8:16] * rows[8 + k] for k, m in enumerate(high))
        return low, high, rhs + scaled * jnp.broadcast_to(innov_wide[pl.ds(channel, 1), :], (LEV, 128))

    def some_channels(index, carry):
        for k in range(8):
            carry = one_channel(8 * index + k, carry)
        return carry

    zero = jnp.zeros((8, 128), F32)
    carry = lax.fori_loop(
        0, CH // 8, some_channels, ((zero,) * LEV, (zero,) * 8, jnp.zeros((LEV, 128), F32))
    )
    for channel in range(CH // 8 * 8, CH):
        carry = one_channel(channel, carry)
    low, high, rhs = carry
    pack_high, pack_low = split(
        jnp.concatenate(list(low) + list(high) + [rhs, jnp.zeros((48, 128), F32)], axis=0)
    )
    packed = dot(chosen, pack_high, NT) + dot(chosen, pack_low, NT)
    for k in range(2):
        for i in range(2):
            send_m[pl.ds(2 * k + i, 128, stride=8), :] = packed[128 * k : 128 * k + 128, 128 * i : 128 * i + 128]
    models = exchange(send_m, recv_m, 8, 4, model_send, model_recv)

    build_table(FY)
    build_table(BY)
    build_table(BX)

    column = iota((8, 128), 1)
    offset = iota((8, 128), 0)

    @pl.loop(0, LEV, unroll=4)
    def _(level):
        taps = line[BX, pl.ds(level, 1), :]
        cov = dot(jnp.broadcast_to(taps, (8, 128)), circulant(taps), NT, precision=HIGHEST)
        ring = pltpu.roll(cov, 64, 1, stride=1, stride_axis=0)
        at = pl.ds(pl.multiple_of(8 * level, 8), 8)
        autocov[0, at, :] = jnp.where(column > offset, ring, 0.0)
        autocov[1, at, :] = jnp.where(column < offset, ring, 0.0)

    dense.wait_recv()

    for block in range(8):
        values = recv_g[256 * block : 256 * block + 256, :].astype(F32).reshape(16, 16, 128)
        wide[128 * block : 128 * block + 128, :] = values[:, 8:16].reshape(128, 128)
        turned = jnp.transpose(values[:, 0:8].reshape(128, 128))
        grid[:, 8 * block : 8 * block + 8, :] = turned.reshape(LEV, 8, 128)

    for k in range(2):
        turned = jnp.transpose(wide[pl.ds(k, 128, stride=8), :])
        cell_x = turned[0:1] - 1.0
        cell_y = jnp.where(cell_x < 0.0, -1.0, 8.0 * turned[1:2] + turned[2:3])
        cells[k : k + 1, :] = cell_x
        cells[2 + k : 3 + k, :] = cell_y
    cells[4:8, :] = jnp.zeros((4, 128), F32)
    place[MIDDLE] = cells[...]

    def neighbour_copy(source, target, send_sem, recv_sem, slot):
        other = (me - (slot - MIDDLE)) & (ND - 1)
        return pltpu.make_async_remote_copy(
            src_ref=source,
            dst_ref=target.at[slot],
            send_sem=send_sem.at[slot],
            recv_sem=recv_sem.at[slot],
            device_id=device(other),
            device_id_type=MESH,
        )

    def for_neighbours(action, unroll=1):
        @pl.loop(0, NEAR - 1, unroll=unroll)
        def _(index):
            action(index + (index >= MIDDLE).astype(I32))

    for_neighbours(lambda slot: neighbour_copy(cells, place, cell_send, cell_recv, slot).start())

    def filter_to_field(level, own):
        out = along_y(own, FY, level)
        for b in range(8):
            high_field[8 * level : 8 * level + 8, 128 * b : 128 * b + 128] = out[8 * b : 8 * b + 8]

    for level in range(LEV):
        filter_to_field(level, grid[level])

    def both(slot, row):
        return jnp.concatenate([place[slot, row : row + 1, :], place[slot, row + 1 : row + 2, :]], axis=1)

    own_rows = both(MIDDLE, 2)
    row_number = iota((128, 256), 0).astype(F32)
    for block in range(8):
        hit = (row_number + float(128 * block)) == own_rows
        onehot_rows[128 * block : 128 * block + 128, :] = hit.astype(BF16)
    own_columns = both(MIDDLE, 0)
    own_column = jnp.broadcast_to(own_columns, (8, 256)) == iota((8, 256), 0).astype(F32)
    own_mask = jnp.broadcast_to(own_column[None], (LEV, 8, 256)).reshape(LEV * 8, 256)

    def sample():
        product = dot(stacked(high_field[...]), onehot_rows[...])
        product = product[:128] + product[128:]
        return jnp.sum(jnp.where(own_column[None], product.reshape(LEV, 8, 256), 0.0), axis=1)

    def apply_model(values):
        lower, upper = values[0:8], values[8:16]
        first = jnp.zeros((8, 256), F32)
        second = jnp.zeros((8, 256), F32)
        cross = []
        for k in range(LEV):
            first = first + model_low[k] * jnp.broadcast_to(values[k : k + 1], (8, 256))
        for k in range(8):
            second = second + model_high[k] * jnp.broadcast_to(upper[k : k + 1], (8, 256))
            cross.append(jnp.sum(model_low[8 + k] * lower, axis=0, keepdims=True))
        return jnp.concatenate([first, second + jnp.concatenate(cross, axis=0)], axis=0)

    z0 = sample()
    models.wait_recv()
    for k in range(2):
        lanes = slice(128 * k, 128 * k + 128)
        turned = jnp.transpose(recv_m[pl.ds(2 * k, 128, stride=8), :])
        model_low[:, :, lanes] = turned.reshape(LEV, 8, 128)
        turned = jnp.transpose(recv_m[pl.ds(2 * k + 1, 128, stride=8), :])
        model_high[:, :, lanes] = turned[0:64].reshape(8, 8, 128)
        extra[:, lanes] = turned[64:80]
    q1 = apply_model(z0) - extra[...]
    queue_a[...] = q1
    recv_a[MIDDLE] = q1
    for_neighbours(lambda slot: neighbour_copy(queue_a, recv_a, qa_send, qa_recv, slot).start())

    lane_number = iota((256, 128), 1).astype(F32)

    def build_onehot(slot):
        base = 256 * slot if isinstance(slot, int) else pl.multiple_of(256 * slot, 256)
        rows = place[slot]
        turned = jnp.transpose(jnp.concatenate([rows] + [jnp.zeros((8, 128), F32)] * 15, axis=0))
        rows_of = jnp.concatenate([turned[:, 2:3], turned[:, 3:4]], axis=0)
        rows_of = jnp.broadcast_to(rows_of, (256, 128))
        for block in range(8):
            hit = (lane_number + float(128 * block)) == rows_of
            onehot[pl.ds(base, 256), 128 * block : 128 * block + 128] = hit.astype(BF16)

        columns_of = both(slot, 0)
        wraps = slot == NEAR - 1
        first = jnp.where(wraps, 0, 8 * slot).astype(F32)
        hit = (row_number == columns_of + first).astype(BF16)
        product = dot(stacked(autocov[jnp.where(wraps, 1, 0)]), hit)
        near_x[slot] = product[:128] + product[128:]

    build_onehot(MIDDLE)

    def from_grid(then):
        for level in range(LEV):
            then(level, along_y(grid[level], BY, level))

    def to_grid(quarter, total):
        total = total[0:128] + total[128:256]
        for half in range(2):
            at = 16 * quarter + 8 * half
            grid[:, at : at + 8, :] = total[:, 128 * half : 128 * half + 128].reshape(LEV, 8, 128)

    def own_adjoint(index, values):
        def keep(level, out):
            adjoint[index, level] = out

        pair = stacked(jnp.where(own_mask, spread_levels(values), 0.0))
        for quarter in range(4):
            hits = onehot[256 * MIDDLE : 256 * MIDDLE + 256, 256 * quarter : 256 * quarter + 256]
            to_grid(quarter, dot(pair, hits))
        from_grid(keep)

    own_adjoint(0, q1)

    def arrive_cells(slot):
        neighbour_copy(cells, place, cell_send, cell_recv, slot).wait_recv()
        build_onehot(slot)

    for_neighbours(arrive_cells)

    groups = ((0, 4), (4, 9), (9, 13), (13, 17))

    def covary(source, target, send_sem, recv_sem, beside):
        for number, (first, last) in enumerate(groups):
            for slot in range(first, last):
                if slot != MIDDLE:
                    neighbour_copy(source, target, send_sem, recv_sem, slot).wait_recv()
                spread_q[:, 256 * slot : 256 * slot + 256] = stacked(near_x[slot] * spread_levels(target[slot]))
            for quarter in range(4):
                total = dot(
                    spread_q[:, 256 * first : 256 * last],
                    onehot[256 * first : 256 * last, 256 * quarter : 256 * quarter + 256],
                )
                if number:
                    total = total + field[quarter]
                if number == len(groups) - 1:
                    to_grid(quarter, total)
                else:
                    field[quarter] = total
            beside(number)
        from_grid(filter_to_field)
        return sample()

    t1 = covary(queue_a, recv_a, qa_send, qa_recv, lambda number: None)
    s0 = -(z0 + t1)
    q2 = apply_model(s0)
    queue_b[...] = q2
    recv_b[MIDDLE] = q2
    for_neighbours(lambda slot: neighbour_copy(queue_b, recv_b, qb_send, qb_recv, slot).start())
    own_adjoint(1, q2)

    def early_tiles(block):
        at = pl.ds(pl.multiple_of(8 * block, 8), 8)
        first, second = [
            swap_groups([adjoint[k, level, at, :] for level in range(LEV)]) for k in range(2)
        ]
        return [jnp.concatenate([first[j], second[j]], axis=0) for j in range(16)]

    def send_early(number):
        for turn in (2 * number, 2 * number + 1):
            store_tiles(early_tiles, send_f, turn)
            send_tiles(send_f, recv_f, 16, turn, early_send, early_recv)

    t2 = covary(queue_b, recv_b, qb_send, qb_recv, send_early)
    keep_own(send_f, recv_f, 16)
    early = all_sent(recv_f, 16, early_send, early_recv)
    u = apply_model(t2)

    own_adjoint(2, u)
    c0c0 = jnp.sum(jnp.sum(c0_ref[...] * c0_ref[...], axis=0))
    lane = iota((1, 128), 1)
    row = jnp.zeros((1, 128), F32)
    for k, value in enumerate(
        (c0c0, jnp.sum(z0 * q1), jnp.sum(q1 * t1), jnp.sum(s0 * q2), jnp.sum(t2 * q2), jnp.sum(t2 * u))
    ):
        row = jnp.where(lane == k, value, row)

    for turn in range(NPX):
        block = (my_x + turn) & (NPX - 1)
        at = pl.ds(pl.multiple_of(8 * block, 8), 8)
        for j, tile in enumerate(swap_groups([adjoint[2, level, at, :] for level in range(LEV)])):
            send_u[pl.ds(pl.multiple_of(256 * block + 16 * j, 16), 8), :] = tile
            send_u[pl.ds(256 * block + 16 * j + 8, 1), :] = row
        send_tiles(send_u, recv_u, 9, turn, final_send, final_recv)
    keep_own(send_u, recv_u, 9)
    final = all_sent(recv_u, 9, final_send, final_recv)

    early.wait_recv()
    for block in range(8):
        arrived = recv_f[256 * block : 256 * block + 256, :].astype(F32).reshape(16, 2, 8, 128)
        for index in range(2):
            turned = jnp.transpose(arrived[:, index].reshape(128, 128))
            adjoint[index, :, 8 * block : 8 * block + 8, :] = turned.reshape(LEV, 8, 128)

    final.wait_recv()
    summed = jnp.sum(recv_u[pl.ds(8, ND, stride=16), :], axis=0, keepdims=True)
    c0c0, z0q1, q1t1, s0q2, q2t2, t2u = [summed[:, k : k + 1] for k in range(6)]
    norm0 = c0c0 + 2.0 * z0q1 + q1t1
    alpha0 = norm0 / (norm0 + s0q2)
    keep = 1.0 - alpha0
    norm1 = keep * keep * norm0 - 2.0 * alpha0 * keep * s0q2 + alpha0 * alpha0 * q2t2
    beta0 = norm1 / norm0
    gain = keep + beta0
    curvature = gain * gain * s0q2 - 2.0 * gain * alpha0 * q2t2 + alpha0 * alpha0 * t2u
    alpha1 = norm1 / (norm1 + beta0 * beta0 * norm0 + curvature)
    coef_c = alpha0 + alpha1 * gain
    coef_r = (1.0 - alpha1) * keep - alpha1 * beta0
    control_2 = alpha0 * alpha1
    residual_2 = (1.0 - alpha1) * alpha0 + alpha1 * gain
    residual_u = -alpha1 * alpha0

    for block in range(8):
        arrived = recv_u[256 * block : 256 * block + 256, :].reshape(16, 16, 128)[:, 0:8]
        turned = jnp.transpose(arrived.reshape(128, 128))
        adjoint[2, :, 8 * block : 8 * block + 8, :] = turned.reshape(LEV, 8, 128)

    for level in range(LEV):
        one, two, three = [adjoint[k, level] for k in range(3)]
        for out_ref, coef, value in (
            (control_ref, 1.0 - coef_c, coef_c * one + control_2 * two),
            (residual_ref, -coef_r, coef_r * one + residual_2 * two + residual_u * three),
        ):
            out = along_x(value, BX, level)
            for b in range(8):
                lanes = slice(128 * b, 128 * b + 128)
                out_ref[level, :, lanes] = coef * c0_ref[level, :, lanes] - out[8 * b : 8 * b + 8]

    dense.wait_send()
    models.wait_send()
    early.wait_send()
    final.wait_send()

    def sent(slot):
        neighbour_copy(cells, place, cell_send, cell_recv, slot).wait_send()
        neighbour_copy(queue_a, recv_a, qa_send, qa_recv, slot).wait_send()
        neighbour_copy(queue_b, recv_b, qb_send, qb_recv, slot).wait_send()

    for_neighbours(sent)


def per_device(
    control_init, kernel_x, kernel_y, obs_weight, jacobian, innovation, obs_dest, obs_cell
):
    vmem = pl.BlockSpec(memory_space=pltpu.VMEM)
    anywhere = pl.BlockSpec(memory_space=pl.ANY)
    shape = jax.ShapeDtypeStruct(control_init.shape, F32)
    dma = pltpu.SemaphoreType.DMA
    return pl.pallas_call(
        kernel,
        out_shape=(shape, shape),
        in_specs=[anywhere] * 8,
        out_specs=(vmem, vmem),
        scratch_shapes=[
            pltpu.VMEM((LEV, 8, 1024), F32),
            pltpu.VMEM((LEV, TAPS), F32),
            pltpu.VMEM((LEV, TAPS), F32),
            pltpu.SMEM((CH,), F32),
            pltpu.VMEM((CH, LEV, 128), BF16),
            pltpu.VMEM((CH, 128), BF16),
            pltpu.VMEM((1, 128), I32),
            pltpu.VMEM((1, 128), I32),
            pltpu.VMEM((CH, 128), F32),
            pltpu.VMEM((4, LEV, 128), F32),
            pltpu.VMEM((4, LEV, 256, 256), BF16),
            pltpu.VMEM((8, LEV, 8, 128), F32),
            pltpu.VMEM((1024, 128), F32),
            pltpu.VMEM((2048, 128), BF16),
            pltpu.VMEM((2048, 128), BF16),
            pltpu.VMEM((1024, 128), F32),
            pltpu.VMEM((1024, 128), F32),
            pltpu.VMEM((1024, 128), F32),
            pltpu.VMEM((LEV, 8, 256), F32),
            pltpu.VMEM((8, 8, 256), F32),
            pltpu.VMEM((LEV, 256), F32),
            pltpu.VMEM((REACH, 1024), BF16),
            pltpu.VMEM((1024, 256), BF16),
            pltpu.VMEM((2, 128, 128), F32),
            pltpu.VMEM((NEAR, 128, 256), F32),
            pltpu.VMEM((NEAR, 8, 128), F32),
            pltpu.VMEM((8, 128), F32),
            pltpu.VMEM((LEV, 256), F32),
            pltpu.VMEM((LEV, 256), F32),
            pltpu.VMEM((NEAR, LEV, 256), F32),
            pltpu.VMEM((NEAR, LEV, 256), F32),
            pltpu.VMEM((256, REACH), BF16),
            pltpu.VMEM((LEV, 64, 128), F32),
            pltpu.VMEM((128, 1024), F32),
            pltpu.VMEM((3, LEV, 64, 128), F32),
            pltpu.VMEM((4, 256, 256), F32),
            pltpu.VMEM((2048, 128), F32),
            pltpu.VMEM((2048, 128), F32),
            pltpu.VMEM((2048, 128), BF16),
            pltpu.VMEM((2048, 128), BF16),
            pltpu.SemaphoreType.REGULAR,
            dma((8,)),
            dma, dma, dma, dma,
            dma((NEAR,)), dma((NEAR,)),
            dma((NEAR,)), dma((NEAR,)), dma((NEAR,)), dma((NEAR,)),
            dma, dma, dma, dma,
        ],
        compiler_params=pltpu.CompilerParams(
            collective_id=0, has_side_effects=True, vmem_limit_bytes=60 * 1024 * 1024
        ),
    )(
        control_init,
        kernel_x,
        kernel_y,
        obs_weight,
        jnp.transpose(jacobian, (2, 1, 0)),
        jnp.transpose(innovation),
        jnp.transpose(obs_dest),
        obs_cell.reshape(1, -1),
    )


def solution(mesh):
    in_specs = (
        P(None, ("px", "py"), None),
        P(),
        P(),
        P(),
        P(("px", "py"), None, None),
        P(("px", "py"), None),
        P(("px", "py"), None),
        P(("px", "py")),
    )
    out_specs = (P(None, ("px", "py"), None), P(None, ("px", "py"), None))
    return jax.shard_map(
        per_device, mesh=mesh, in_specs=in_specs, out_specs=out_specs, check_vma=False
    )
```

```python
import functools

import jax
import jax.numpy as jnp
from jax import lax
from jax.experimental import pallas as pl
from jax.experimental.pallas import tpu as pltpu
from jax.sharding import PartitionSpec as P

F32, BF16, I32 = jnp.float32, jnp.bfloat16, jnp.int32
MESH = pl.DeviceIdType.MESH
ND, NPX, NPY = 128, 8, 16
LEV, CH, TAPS = 16, 431, 64
NEAR = 17
MIDDLE = 8
REACH = NEAR * 256
FX, BX, FY, BY = range(4)
NT = (((1,), (1,)), ((), ()))
NN = (((1,), (0,)), ((), ()))
HIGHEST = lax.Precision.HIGHEST


def iota(shape, axis):
    return lax.broadcasted_iota(I32, shape, axis)


def split(values):
    high = values.astype(BF16)
    low = (values - high.astype(F32)).astype(BF16)
    return high, low


def stacked(values):
    return jnp.concatenate(split(values), axis=0)


def dot(left, right, dims=NN, precision=None):
    return lax.dot_general(left, right, dims, precision=precision, preferred_element_type=F32)


def swap_groups(tiles):
    group = iota((8, 128), 1) // 8
    tiles = list(tiles)
    for bit in range(4):
        step = 1 << bit
        upper = (group & step) != 0
        for a in range(16):
            if a & step == 0:
                first, second = tiles[a], tiles[a + step]
                tiles[a] = jnp.where(upper, pltpu.roll(second, 8 * step, 1), first)
                tiles[a + step] = jnp.where(upper, second, pltpu.roll(first, 128 - 8 * step, 1))
    return tiles


def spread_levels(values):
    count = values.shape[1]
    return jnp.broadcast_to(values[:, None, :], (LEV, 8, count)).reshape(LEV * 8, count)


def kernel(
    c0_hbm, kx_hbm, ky_hbm, w_hbm, jac_hbm, innov_hbm, dest_hbm, cell_hbm,
    control_hbm, residual_hbm,
    c0_ref, kx_ref, ky_ref, w_ref, jac, innov, dest_ref, cell_ref,
    innov_wide, line, table, mixed, tile_m, send_g, recv_g, wide, send_m, recv_m,
    model_low, model_high, extra, onehot, onehot_rows, autocov, near_x, place, cells, queue_a, queue_b,
    recv_a, recv_b, spread_q, grid, high_field, adjoint, field, change, send_u, recv_u, send_f, recv_f,
    entered, load_sem, store_sem, model_send, model_recv, dense_send, dense_recv, cell_send, cell_recv,
    qa_send, qa_recv, qb_send, qb_recv, early_send, early_recv, final_send, final_recv,
):
    my_x, my_y = lax.axis_index("px"), lax.axis_index("py")
    me = my_x * NPY + my_y

    def device(index):
        return (index >> 4, index & 15)

    loads = [
        pltpu.make_async_copy(source, target, load_sem.at[i])
        for i, (source, target) in enumerate(
            (
                (c0_hbm, c0_ref), (kx_hbm, kx_ref), (ky_hbm, ky_ref), (w_hbm, w_ref),
                (jac_hbm, jac), (innov_hbm, innov), (dest_hbm, dest_ref), (cell_hbm, cell_ref),
            )
        )
    ]
    for load in loads:
        load.start()

    barrier = pltpu.get_barrier_semaphore()

    for step in range(1, NPY):
        pl.semaphore_signal(
            barrier, inc=1, device_id=(my_x, (my_y + step) & (NPY - 1)), device_id_type=MESH
        )
    for step in range(1, NPX):
        pl.semaphore_signal(
            barrier, inc=1, device_id=((my_x + step) & (NPX - 1), my_y), device_id_type=MESH
        )

    loads[1].wait()
    loads[2].wait()
    tap = iota((TAPS, 128), 0)
    place_at = iota((TAPS, 128), 1)
    pick_forward = (tap == ((32 - place_at) & 127)).astype(F32)
    pick_backward = (tap == ((place_at + 32) & 127)).astype(F32)
    for which, (taps_ref, pick) in enumerate(
        ((kx_ref, pick_forward), (kx_ref, pick_backward), (ky_ref, pick_forward), (ky_ref, pick_backward))
    ):
        line[which] = dot(taps_ref[...], pick, precision=HIGHEST)

    inside = jnp.abs(iota((128, 128), 0) - iota((128, 128), 1)) < 64

    def circulant(row):
        return pltpu.roll(jnp.broadcast_to(row, (128, 128)), 0, 1, stride=1, stride_axis=0)

    def build_table(which):
        @pl.loop(0, LEV, unroll=4)
        def _(level):
            ring = circulant(line[which, pl.ds(level, 1), :])
            high, low = split(ring)
            pair = jnp.concatenate([high, low], axis=1)
            nil = jnp.zeros((), BF16)
            keep = jnp.concatenate([inside, inside], axis=1)
            table[which, level, 0:128, :] = jnp.where(keep, pair, nil)
            table[which, level, 128:256, :] = jnp.where(keep, nil, pair)

    def convolve(own, before, after, which, level):
        count = own.shape[0]
        beside = jnp.where(iota((count, 128), 1) < 64, after, before)
        product = dot(stacked(jnp.concatenate([own, beside], axis=1)), table[which, level])
        upper, lower = product[:count], product[count:]
        return (upper[:, :128] + upper[:, 128:]) + (lower[:, :128] + lower[:, 128:])

    def along_x(own, which, level):
        before = jnp.concatenate([own[56:], own[:56]], axis=0)
        after = jnp.concatenate([own[8:], own[:8]], axis=0)
        return convolve(own, before, after, which, level)

    edge = jnp.zeros((8, 128), F32)

    def along_y(own, which, level):
        before = jnp.concatenate([edge, own[:56]], axis=0)
        after = jnp.concatenate([own[8:], edge], axis=0)
        return convolve(own, before, after, which, level)

    build_table(FX)
    loads[0].wait()

    for level in range(LEV):
        own = jnp.concatenate([c0_ref[level, :, 128 * b : 128 * b + 128] for b in range(8)], axis=0)
        out = along_x(own, FX, level)
        for b in range(8):
            mixed[b, level] = out[8 * b : 8 * b + 8]

    loads[6].wait()
    loads[7].wait()
    cell = cell_ref[...]
    codes = jnp.concatenate([(cell >> 10) + 1, (cell & 1023) >> 3, cell & 7, jnp.zeros((125, 128), I32)], axis=0)
    dest = jnp.broadcast_to(dest_ref[...], (128, 128))
    dest_t = jnp.transpose(dest.astype(F32))
    earlier = (dest.astype(F32) == dest_t) & (iota((128, 128), 0) < iota((128, 128), 1))
    rank = jnp.sum(earlier.astype(F32), axis=0, keepdims=True)
    named = iota((128, 128), 0) == dest
    chosen = jnp.concatenate([(named & (rank == float(k))).astype(BF16) for k in range(2)], axis=0)
    packed = dot(chosen, codes.astype(F32).astype(BF16), NT)
    for k in range(2):
        tile_m[pl.ds(k, 128, stride=8), :] = packed[128 * k : 128 * k + 128]
    for i in range(2, 8):
        tile_m[pl.ds(i, 128, stride=8), :] = jnp.zeros((128, 128), F32)

    pl.semaphore_wait(barrier, NPX + NPY - 2)
    for step in range(1, NPX):
        pl.semaphore_signal(
            entered, inc=1, device_id=((my_x + step) & (NPX - 1), my_y), device_id_type=MESH
        )
    def send_one(source, target, rows, other, source_rows, send_sem, recv_sem):
        pltpu.make_async_remote_copy(
            src_ref=source.at[source_rows],
            dst_ref=target.at[rows],
            send_sem=send_sem,
            recv_sem=recv_sem,
            device_id=device(other),
            device_id_type=MESH,
        ).start()

    def all_sent(target, rows, send_sem, recv_sem):
        whole = pl.ds(0, (ND - 1) * rows)
        return pltpu.make_async_remote_copy(
            src_ref=target.at[whole],
            dst_ref=target.at[whole],
            send_sem=send_sem,
            recv_sem=recv_sem,
            device_id=device((me + 1) & (ND - 1)),
            device_id_type=MESH,
        )

    def rows_of(index, stride, count):
        return pl.ds(pl.multiple_of(index * stride, stride), count)

    def store_tiles(tiles, source, turn):
        block = (my_x + turn) & (NPX - 1)
        for j, tile in enumerate(tiles(block)):
            source[pl.ds(pl.multiple_of(256 * block + 16 * j, 16), 16), :] = tile.astype(BF16)

    def send_tiles(source, target, rows, turn, send_sem, recv_sem):
        mine = rows_of(me, 16, rows)
        block = (my_x + turn) & (NPX - 1)
        for j in range(1 if turn == 0 else 0, NPY):
            other = block * NPY + ((my_y + j) & (NPY - 1))
            send_one(source, target, mine, other, rows_of(other, 16, rows), send_sem, recv_sem)

    def keep_own(source, target, rows):
        mine = rows_of(me, 16, rows)
        target[mine, :] = source[mine, :]

    def first_tiles(block):
        tiles = swap_groups([mixed[block, level] for level in range(LEV)])
        lower = [tile_m[pl.ds(pl.multiple_of(128 * block + 8 * j, 8), 8), :] for j in range(16)]
        return [jnp.concatenate([tiles[j], lower[j]], axis=0) for j in range(16)]

    for turn in range(NPX):
        store_tiles(first_tiles, send_g, turn)
    send_tiles(send_g, recv_g, 16, 0, dense_send, dense_recv)
    pl.semaphore_wait(entered, NPX - 1)
    for turn in range(1, NPX):
        send_tiles(send_g, recv_g, 16, turn, dense_send, dense_recv)
    keep_own(send_g, recv_g, 16)
    dense = all_sent(recv_g, 16, dense_send, dense_recv)

    for load in loads[3:6]:
        load.wait()
    innov_wide[...] = innov[...].astype(F32)

    def one_channel(channel, carry):
        values = jac[channel].astype(F32)
        scaled = values * w_ref[channel]
        low, high, rhs = carry
        rows = [jnp.broadcast_to(values[k : k + 1], (8, 128)) for k in range(LEV)]
        low = tuple(m + scaled[0:8] * rows[k] for k, m in enumerate(low))
        high = tuple(m + scaled[8:16] * rows[8 + k] for k, m in enumerate(high))
        return low, high, rhs + scaled * jnp.broadcast_to(innov_wide[pl.ds(channel, 1), :], (LEV, 128))

    def some_channels(index, carry):
        for k in range(8):
            carry = one_channel(8 * index + k, carry)
        return carry

    zero = jnp.zeros((8, 128), F32)
    carry = lax.fori_loop(
        0, CH // 8, some_channels, ((zero,) * LEV, (zero,) * 8, jnp.zeros((LEV, 128), F32))
    )
    for channel in range(CH // 8 * 8, CH):
        carry = one_channel(channel, carry)
    low, high, rhs = carry
    pack_high, pack_low = split(
        jnp.concatenate(list(low) + list(high) + [rhs, jnp.zeros((48, 128), F32)], axis=0)
    )
    packed = dot(chosen, pack_high, NT) + dot(chosen, pack_low, NT)
    for k in range(2):
        for i in range(2):
            send_m[pl.ds(2 * k + i, 128, stride=8), :] = packed[128 * k : 128 * k + 128, 128 * i : 128 * i + 128]
    own_rows = rows_of(me, 8, 4)

    def send_model(step):
        other = (me + step) & (ND - 1)
        send_one(send_m, recv_m, own_rows, other, rows_of(other, 8, 4), model_send, model_recv)

    @pl.loop(1, ND)
    def _(step):
        send_model(step)

    recv_m[own_rows, :] = send_m[own_rows, :]
    models = all_sent(recv_m, 4, model_send, model_recv)

    build_table(FY)
    build_table(BY)
    build_table(BX)

    column = iota((8, 128), 1)
    offset = iota((8, 128), 0)

    @pl.loop(0, LEV, unroll=4)
    def _(level):
        taps = line[BX, pl.ds(level, 1), :]
        cov = dot(jnp.broadcast_to(taps, (8, 128)), circulant(taps), NT, precision=HIGHEST)
        ring = pltpu.roll(cov, 64, 1, stride=1, stride_axis=0)
        at = pl.ds(pl.multiple_of(8 * level, 8), 8)
        autocov[0, at, :] = jnp.where(column > offset, ring, 0.0)
        autocov[1, at, :] = jnp.where(column < offset, ring, 0.0)

    dense.wait_recv()

    for block in range(8):
        values = recv_g[256 * block : 256 * block + 256, :].astype(F32).reshape(16, 16, 128)
        wide[128 * block : 128 * block + 128, :] = values[:, 8:16].reshape(128, 128)
        turned = jnp.transpose(values[:, 0:8].reshape(128, 128))
        grid[:, 8 * block : 8 * block + 8, :] = turned.reshape(LEV, 8, 128)

    for k in range(2):
        turned = jnp.transpose(wide[pl.ds(k, 128, stride=8), :])
        cell_x = turned[0:1] - 1.0
        cell_y = jnp.where(cell_x < 0.0, -1.0, 8.0 * turned[1:2] + turned[2:3])
        cells[k : k + 1, :] = cell_x
        cells[2 + k : 3 + k, :] = cell_y
    cells[4:8, :] = jnp.zeros((4, 128), F32)
    place[MIDDLE] = cells[...]

    def neighbour_copy(source, target, send_sem, recv_sem, slot):
        other = (me - (slot - MIDDLE)) & (ND - 1)
        return pltpu.make_async_remote_copy(
            src_ref=source,
            dst_ref=target.at[slot],
            send_sem=send_sem.at[slot],
            recv_sem=recv_sem.at[slot],
            device_id=device(other),
            device_id_type=MESH,
        )

    def for_neighbours(action, unroll=1):
        @pl.loop(0, NEAR - 1, unroll=unroll)
        def _(index):
            action(index + (index >= MIDDLE).astype(I32))

    for_neighbours(lambda slot: neighbour_copy(cells, place, cell_send, cell_recv, slot).start())

    def filter_to_field(level, own):
        out = along_y(own, FY, level)
        for b in range(8):
            high_field[8 * level : 8 * level + 8, 128 * b : 128 * b + 128] = out[8 * b : 8 * b + 8]

    for level in range(LEV):
        filter_to_field(level, grid[level])

    def both(slot, row):
        return jnp.concatenate([place[slot, row : row + 1, :], place[slot, row + 1 : row + 2, :]], axis=1)

    own_rows = both(MIDDLE, 2)
    row_number = iota((128, 256), 0).astype(F32)
    for block in range(8):
        hit = (row_number + float(128 * block)) == own_rows
        onehot_rows[128 * block : 128 * block + 128, :] = hit.astype(BF16)
    own_columns = both(MIDDLE, 0)
    own_column = jnp.broadcast_to(own_columns, (8, 256)) == iota((8, 256), 0).astype(F32)
    own_mask = jnp.broadcast_to(own_column[None], (LEV, 8, 256)).reshape(LEV * 8, 256)

    def sample():
        product = dot(stacked(high_field[...]), onehot_rows[...])
        product = product[:128] + product[128:]
        return jnp.sum(jnp.where(own_column[None], product.reshape(LEV, 8, 256), 0.0), axis=1)

    def apply_model(values):
        lower, upper = values[0:8], values[8:16]
        first = jnp.zeros((8, 256), F32)
        second = jnp.zeros((8, 256), F32)
        cross = []
        for k in range(LEV):
            first = first + model_low[k] * jnp.broadcast_to(values[k : k + 1], (8, 256))
        for k in range(8):
            second = second + model_high[k] * jnp.broadcast_to(upper[k : k + 1], (8, 256))
            cross.append(jnp.sum(model_low[8 + k] * lower, axis=0, keepdims=True))
        return jnp.concatenate([first, second + jnp.concatenate(cross, axis=0)], axis=0)

    z0 = sample()
    models.wait_recv()
    for k in range(2):
        lanes = slice(128 * k, 128 * k + 128)
        turned = jnp.transpose(recv_m[pl.ds(2 * k, 128, stride=8), :])
        model_low[:, :, lanes] = turned.reshape(LEV, 8, 128)
        turned = jnp.transpose(recv_m[pl.ds(2 * k + 1, 128, stride=8), :])
        model_high[:, :, lanes] = turned[0:64].reshape(8, 8, 128)
        extra[:, lanes] = turned[64:80]
    q1 = apply_model(z0) - extra[...]
    queue_a[...] = q1
    recv_a[MIDDLE] = q1
    for_neighbours(lambda slot: neighbour_copy(queue_a, recv_a, qa_send, qa_recv, slot).start())

    lane_number = iota((256, 128), 1).astype(F32)

    def build_onehot(slot):
        base = 256 * slot if isinstance(slot, int) else pl.multiple_of(256 * slot, 256)
        rows = place[slot]
        turned = jnp.transpose(jnp.concatenate([rows] + [jnp.zeros((8, 128), F32)] * 15, axis=0))
        rows_of = jnp.concatenate([turned[:, 2:3], turned[:, 3:4]], axis=0)
        rows_of = jnp.broadcast_to(rows_of, (256, 128))
        for block in range(8):
            hit = (lane_number + float(128 * block)) == rows_of
            onehot[pl.ds(base, 256), 128 * block : 128 * block + 128] = hit.astype(BF16)

        columns_of = both(slot, 0)
        wraps = slot == NEAR - 1
        first = jnp.where(wraps, 0, 8 * slot).astype(F32)
        hit = (row_number == columns_of + first).astype(BF16)
        product = dot(stacked(autocov[jnp.where(wraps, 1, 0)]), hit)
        near_x[slot] = product[:128] + product[128:]

    build_onehot(MIDDLE)

    def from_grid(then):
        for level in range(LEV):
            then(level, along_y(grid[level], BY, level))

    def to_grid(quarter, total):
        total = total[0:128] + total[128:256]
        for half in range(2):
            at = 16 * quarter + 8 * half
            grid[:, at : at + 8, :] = total[:, 128 * half : 128 * half + 128].reshape(LEV, 8, 128)

    def own_adjoint(index, values):
        def keep(level, out):
            adjoint[index, level] = out

        pair = stacked(jnp.where(own_mask, spread_levels(values), 0.0))
        for quarter in range(4):
            hits = onehot[256 * MIDDLE : 256 * MIDDLE + 256, 256 * quarter : 256 * quarter + 256]
            to_grid(quarter, dot(pair, hits))
        from_grid(keep)

    own_adjoint(0, q1)

    def arrive_cells(slot):
        neighbour_copy(cells, place, cell_send, cell_recv, slot).wait_recv()
        build_onehot(slot)

    for_neighbours(arrive_cells)

    groups = ((0, 4), (4, 9), (9, 13), (13, 17))

    def covary(source, target, send_sem, recv_sem, beside):
        for number, (first, last) in enumerate(groups):
            for slot in range(first, last):
                if slot != MIDDLE:
                    neighbour_copy(source, target, send_sem, recv_sem, slot).wait_recv()
                spread_q[:, 256 * slot : 256 * slot + 256] = stacked(near_x[slot] * spread_levels(target[slot]))
            for quarter in range(4):
                total = dot(
                    spread_q[:, 256 * first : 256 * last],
                    onehot[256 * first : 256 * last, 256 * quarter : 256 * quarter + 256],
                )
                if number:
                    total = total + field[quarter]
                if number == len(groups) - 1:
                    to_grid(quarter, total)
                else:
                    field[quarter] = total
            beside(number)
        from_grid(filter_to_field)
        return sample()

    t1 = covary(queue_a, recv_a, qa_send, qa_recv, lambda number: None)
    s0 = -(z0 + t1)
    q2 = apply_model(s0)
    queue_b[...] = q2
    recv_b[MIDDLE] = q2
    for_neighbours(lambda slot: neighbour_copy(queue_b, recv_b, qb_send, qb_recv, slot).start())
    own_adjoint(1, q2)

    def early_tiles(block):
        at = pl.ds(pl.multiple_of(8 * block, 8), 8)
        first, second = [
            swap_groups([adjoint[k, level, at, :] for level in range(LEV)]) for k in range(2)
        ]
        return [jnp.concatenate([first[j], second[j]], axis=0) for j in range(16)]

    def send_early(number):
        for turn in (2 * number, 2 * number + 1):
            send_tiles(send_f, recv_f, 16, turn, early_send, early_recv)

    for turn in range(NPX):
        store_tiles(early_tiles, send_f, turn)
    keep_own(send_f, recv_f, 16)
    lane = iota((1, 128), 1)

    def place_sums(row, first, values):
        for k, value in enumerate(values):
            row = jnp.where(lane == first + k, value, row)
        return row

    c0c0 = jnp.sum(jnp.sum(c0_ref[...] * c0_ref[...], axis=0))
    row = place_sums(
        jnp.zeros((1, 128), F32), 0, (c0c0, jnp.sum(z0 * q1), jnp.sum(q1 * t1), jnp.sum(s0 * q2))
    )
    t2 = covary(queue_b, recv_b, qb_send, qb_recv, send_early)
    early = all_sent(recv_f, 16, early_send, early_recv)
    u = apply_model(t2)

    own_adjoint(2, u)
    row = place_sums(row, 4, (jnp.sum(t2 * q2), jnp.sum(t2 * u)))

    for turn in range(NPX):
        block = (my_x + turn) & (NPX - 1)
        at = pl.ds(pl.multiple_of(8 * block, 8), 8)
        for j, tile in enumerate(swap_groups([adjoint[2, level, at, :] for level in range(LEV)])):
            send_u[pl.ds(pl.multiple_of(256 * block + 16 * j, 16), 8), :] = tile
            send_u[pl.ds(256 * block + 16 * j + 8, 1), :] = row
        send_tiles(send_u, recv_u, 9, turn, final_send, final_recv)
    keep_own(send_u, recv_u, 9)
    final = all_sent(recv_u, 9, final_send, final_recv)

    early.wait_recv()
    for block in range(8):
        arrived = recv_f[256 * block : 256 * block + 256, :].astype(F32).reshape(16, 2, 8, 128)
        for index in range(2):
            turned = jnp.transpose(arrived[:, index].reshape(128, 128))
            adjoint[index, :, 8 * block : 8 * block + 8, :] = turned.reshape(LEV, 8, 128)

    final.wait_recv()
    summed = jnp.sum(recv_u[pl.ds(8, ND, stride=16), :], axis=0, keepdims=True)
    c0c0, z0q1, q1t1, s0q2, q2t2, t2u = [summed[:, k : k + 1] for k in range(6)]
    norm0 = c0c0 + 2.0 * z0q1 + q1t1
    alpha0 = norm0 / (norm0 + s0q2)
    keep = 1.0 - alpha0
    norm1 = keep * keep * norm0 - 2.0 * alpha0 * keep * s0q2 + alpha0 * alpha0 * q2t2
    beta0 = norm1 / norm0
    gain = keep + beta0
    curvature = gain * gain * s0q2 - 2.0 * gain * alpha0 * q2t2 + alpha0 * alpha0 * t2u
    alpha1 = norm1 / (norm1 + beta0 * beta0 * norm0 + curvature)
    coef_c = alpha0 + alpha1 * gain
    coef_r = (1.0 - alpha1) * keep - alpha1 * beta0
    control_2 = alpha0 * alpha1
    residual_2 = (1.0 - alpha1) * alpha0 + alpha1 * gain
    residual_u = -alpha1 * alpha0

    for block in range(8):
        arrived = recv_u[256 * block : 256 * block + 256, :].reshape(16, 16, 128)[:, 0:8]
        turned = jnp.transpose(arrived.reshape(128, 128))
        adjoint[2, :, 8 * block : 8 * block + 8, :] = turned.reshape(LEV, 8, 128)

    for level in range(LEV):
        one, two, three = [adjoint[k, level] for k in range(3)]
        for index, coef, value in (
            (0, -coef_c, coef_c * one + control_2 * two),
            (1, 1.0 - coef_r, coef_r * one + residual_2 * two + residual_u * three),
        ):
            out = along_x(value, BX, level)
            for b in range(8):
                lanes = slice(128 * b, 128 * b + 128)
                change[index, level, :, lanes] = coef * c0_ref[level, :, lanes] - out[8 * b : 8 * b + 8]
            pltpu.make_async_copy(
                change.at[index, level], (control_hbm, residual_hbm)[index].at[level], store_sem.at[index]
            ).start()

    for index, target in enumerate((control_hbm, residual_hbm)):
        pltpu.make_async_copy(change.at[index], target, store_sem.at[index]).wait()

    dense.wait_send()
    models.wait_send()
    early.wait_send()
    final.wait_send()

    def sent(slot):
        neighbour_copy(cells, place, cell_send, cell_recv, slot).wait_send()
        neighbour_copy(queue_a, recv_a, qa_send, qa_recv, slot).wait_send()
        neighbour_copy(queue_b, recv_b, qb_send, qb_recv, slot).wait_send()

    for_neighbours(sent)


def per_device(
    control_init, kernel_x, kernel_y, obs_weight, jacobian, innovation, obs_dest, obs_cell
):
    anywhere = pl.BlockSpec(memory_space=pl.ANY)
    shape = jax.ShapeDtypeStruct(control_init.shape, F32)
    dma = pltpu.SemaphoreType.DMA
    change, shifted = pl.pallas_call(
        kernel,
        out_shape=(shape, shape),
        in_specs=[anywhere] * 8,
        out_specs=(anywhere, anywhere),
        scratch_shapes=[
            pltpu.VMEM((LEV, 8, 1024), F32),
            pltpu.VMEM((LEV, TAPS), F32),
            pltpu.VMEM((LEV, TAPS), F32),
            pltpu.SMEM((CH,), F32),
            pltpu.VMEM((CH, LEV, 128), BF16),
            pltpu.VMEM((CH, 128), BF16),
            pltpu.VMEM((1, 128), I32),
            pltpu.VMEM((1, 128), I32),
            pltpu.VMEM((CH, 128), F32),
            pltpu.VMEM((4, LEV, 128), F32),
            pltpu.VMEM((4, LEV, 256, 256), BF16),
            pltpu.VMEM((8, LEV, 8, 128), F32),
            pltpu.VMEM((1024, 128), F32),
            pltpu.VMEM((2048, 128), BF16),
            pltpu.VMEM((2048, 128), BF16),
            pltpu.VMEM((1024, 128), F32),
            pltpu.VMEM((1024, 128), F32),
            pltpu.VMEM((1024, 128), F32),
            pltpu.VMEM((LEV, 8, 256), F32),
            pltpu.VMEM((8, 8, 256), F32),
            pltpu.VMEM((LEV, 256), F32),
            pltpu.VMEM((REACH, 1024), BF16),
            pltpu.VMEM((1024, 256), BF16),
            pltpu.VMEM((2, 128, 128), F32),
            pltpu.VMEM((NEAR, 128, 256), F32),
            pltpu.VMEM((NEAR, 8, 128), F32),
            pltpu.VMEM((8, 128), F32),
            pltpu.VMEM((LEV, 256), F32),
            pltpu.VMEM((LEV, 256), F32),
            pltpu.VMEM((NEAR, LEV, 256), F32),
            pltpu.VMEM((NEAR, LEV, 256), F32),
            pltpu.VMEM((256, REACH), BF16),
            pltpu.VMEM((LEV, 64, 128), F32),
            pltpu.VMEM((128, 1024), F32),
            pltpu.VMEM((3, LEV, 64, 128), F32),
            pltpu.VMEM((4, 256, 256), F32),
            pltpu.VMEM((2, LEV, 8, 1024), F32),
            pltpu.VMEM((2048, 128), F32),
            pltpu.VMEM((2048, 128), F32),
            pltpu.VMEM((2048, 128), BF16),
            pltpu.VMEM((2048, 128), BF16),
            pltpu.SemaphoreType.REGULAR,
            dma((8,)), dma((2,)),
            dma, dma, dma, dma,
            dma((NEAR,)), dma((NEAR,)),
            dma((NEAR,)), dma((NEAR,)), dma((NEAR,)), dma((NEAR,)),
            dma, dma, dma, dma,
        ],
        compiler_params=pltpu.CompilerParams(
            collective_id=0, has_side_effects=True, vmem_limit_bytes=60 * 1024 * 1024
        ),
    )(
        control_init,
        kernel_x,
        kernel_y,
        obs_weight,
        jnp.transpose(jacobian, (2, 1, 0)),
        jnp.transpose(innovation),
        jnp.transpose(obs_dest),
        obs_cell.reshape(1, -1),
    )
    return control_init + change, shifted - control_init


def solution(mesh):
    in_specs = (
        P(None, ("px", "py"), None),
        P(),
        P(),
        P(),
        P(("px", "py"), None, None),
        P(("px", "py"), None),
        P(("px", "py"), None),
        P(("px", "py")),
    )
    out_specs = (P(None, ("px", "py"), None), P(None, ("px", "py"), None))
    return jax.shard_map(
        per_device, mesh=mesh, in_specs=in_specs, out_specs=out_specs, check_vma=False
    )
```

```python
import functools

import jax
import jax.numpy as jnp
from jax import lax
from jax.experimental import pallas as pl
from jax.experimental.pallas import tpu as pltpu
from jax.sharding import PartitionSpec as P

F32, BF16, I32 = jnp.float32, jnp.bfloat16, jnp.int32
MESH = pl.DeviceIdType.MESH
ND, NPX, NPY = 128, 8, 16
LEV, CH, TAPS = 16, 431, 64
NEAR = 17
MIDDLE = 8
REACH = NEAR * 256
FX, BX, FY, BY = range(4)
NT = (((1,), (1,)), ((), ()))
NN = (((1,), (0,)), ((), ()))
HIGHEST = lax.Precision.HIGHEST


def iota(shape, axis):
    return lax.broadcasted_iota(I32, shape, axis)


def split(values):
    high = values.astype(BF16)
    low = (values - high.astype(F32)).astype(BF16)
    return high, low


def stacked(values):
    return jnp.concatenate(split(values), axis=0)


def dot(left, right, dims=NN, precision=None):
    return lax.dot_general(left, right, dims, precision=precision, preferred_element_type=F32)


def swap_groups(tiles):
    group = iota((8, 128), 1) // 8
    tiles = list(tiles)
    for bit in range(4):
        step = 1 << bit
        upper = (group & step) != 0
        for a in range(16):
            if a & step == 0:
                first, second = tiles[a], tiles[a + step]
                tiles[a] = jnp.where(upper, pltpu.roll(second, 8 * step, 1), first)
                tiles[a + step] = jnp.where(upper, second, pltpu.roll(first, 128 - 8 * step, 1))
    return tiles


def spread_levels(values):
    count = values.shape[1]
    return jnp.broadcast_to(values[:, None, :], (LEV, 8, count)).reshape(LEV * 8, count)


def kernel(
    c0_hbm, kx_hbm, ky_hbm, w_hbm, jac_hbm, innov_hbm, dest_hbm, cell_hbm,
    control_hbm, residual_hbm,
    c0_ref, kx_ref, ky_ref, w_ref, jac, innov, dest_ref, cell_ref,
    innov_wide, line, table, mixed, tile_m, send_g, recv_g, wide, send_m, recv_m,
    model_low, model_high, extra, onehot, onehot_rows, autocov, near_x, place, cells, queue_a, queue_b,
    recv_a, recv_b, spread_q, grid, high_field, adjoint, field, change, send_u, recv_u, send_f, recv_f,
    entered, load_sem, store_sem, model_send, model_recv, dense_send, dense_recv, cell_send, cell_recv,
    qa_send, qa_recv, qb_send, qb_recv, early_send, early_recv, final_send, final_recv,
):
    my_x, my_y = lax.axis_index("px"), lax.axis_index("py")
    me = my_x * NPY + my_y

    def device(index):
        return (index >> 4, index & 15)

    loads = [
        pltpu.make_async_copy(source, target, load_sem.at[i])
        for i, (source, target) in enumerate(
            (
                (c0_hbm, c0_ref), (kx_hbm, kx_ref), (ky_hbm, ky_ref), (w_hbm, w_ref),
                (jac_hbm, jac), (innov_hbm, innov), (dest_hbm, dest_ref), (cell_hbm, cell_ref),
            )
        )
    ]
    for load in loads:
        load.start()

    barrier = pltpu.get_barrier_semaphore()

    for step in range(1, NPY):
        pl.semaphore_signal(
            barrier, inc=1, device_id=(my_x, (my_y + step) & (NPY - 1)), device_id_type=MESH
        )
    for step in range(1, NPX):
        pl.semaphore_signal(
            barrier, inc=1, device_id=((my_x + step) & (NPX - 1), my_y), device_id_type=MESH
        )

    loads[1].wait()
    loads[2].wait()
    tap = iota((TAPS, 128), 0)
    place_at = iota((TAPS, 128), 1)
    pick_forward = (tap == ((32 - place_at) & 127)).astype(F32)
    pick_backward = (tap == ((place_at + 32) & 127)).astype(F32)
    for which, (taps_ref, pick) in enumerate(
        ((kx_ref, pick_forward), (kx_ref, pick_backward), (ky_ref, pick_forward), (ky_ref, pick_backward))
    ):
        line[which] = dot(taps_ref[...], pick, precision=HIGHEST)

    inside = jnp.abs(iota((128, 128), 0) - iota((128, 128), 1)) < 64

    def circulant(row):
        return pltpu.roll(jnp.broadcast_to(row, (128, 128)), 0, 1, stride=1, stride_axis=0)

    def build_table(which):
        @pl.loop(0, LEV, unroll=4)
        def _(level):
            ring = circulant(line[which, pl.ds(level, 1), :])
            high, low = split(ring)
            pair = jnp.concatenate([high, low], axis=1)
            nil = jnp.zeros((), BF16)
            keep = jnp.concatenate([inside, inside], axis=1)
            table[which, level, 0:128, :] = jnp.where(keep, pair, nil)
            table[which, level, 128:256, :] = jnp.where(keep, nil, pair)

    def convolve(own, before, after, which, level):
        count = own.shape[0]
        beside = jnp.where(iota((count, 128), 1) < 64, after, before)
        product = dot(stacked(jnp.concatenate([own, beside], axis=1)), table[which, level])
        upper, lower = product[:count], product[count:]
        return (upper[:, :128] + upper[:, 128:]) + (lower[:, :128] + lower[:, 128:])

    def along_x(own, which, level):
        before = jnp.concatenate([own[56:], own[:56]], axis=0)
        after = jnp.concatenate([own[8:], own[:8]], axis=0)
        return convolve(own, before, after, which, level)

    edge = jnp.zeros((8, 128), F32)

    def along_y(own, which, level):
        before = jnp.concatenate([edge, own[:56]], axis=0)
        after = jnp.concatenate([own[8:], edge], axis=0)
        return convolve(own, before, after, which, level)

    build_table(FX)
    loads[0].wait()

    for level in range(LEV):
        own = jnp.concatenate([c0_ref[level, :, 128 * b : 128 * b + 128] for b in range(8)], axis=0)
        out = along_x(own, FX, level)
        for b in range(8):
            mixed[b, level] = out[8 * b : 8 * b + 8]

    loads[6].wait()
    loads[7].wait()
    cell = cell_ref[...]
    codes = jnp.concatenate([(cell >> 10) + 1, (cell & 1023) >> 3, cell & 7, jnp.zeros((125, 128), I32)], axis=0)
    dest = jnp.broadcast_to(dest_ref[...], (128, 128))
    dest_t = jnp.transpose(dest.astype(F32))
    earlier = (dest.astype(F32) == dest_t) & (iota((128, 128), 0) < iota((128, 128), 1))
    rank = jnp.sum(earlier.astype(F32), axis=0, keepdims=True)
    named = iota((128, 128), 0) == dest
    chosen = jnp.concatenate([(named & (rank == float(k))).astype(BF16) for k in range(2)], axis=0)
    packed = dot(chosen, codes.astype(F32).astype(BF16), NT)
    for k in range(2):
        tile_m[pl.ds(k, 128, stride=8), :] = packed[128 * k : 128 * k + 128]
    for i in range(2, 8):
        tile_m[pl.ds(i, 128, stride=8), :] = jnp.zeros((128, 128), F32)

    pl.semaphore_wait(barrier, NPX + NPY - 2)
    for step in range(1, NPX):
        pl.semaphore_signal(
            entered, inc=1, device_id=((my_x + step) & (NPX - 1), my_y), device_id_type=MESH
        )
    def send_one(source, target, rows, other, source_rows, send_sem, recv_sem):
        pltpu.make_async_remote_copy(
            src_ref=source.at[source_rows],
            dst_ref=target.at[rows],
            send_sem=send_sem,
            recv_sem=recv_sem,
            device_id=device(other),
            device_id_type=MESH,
        ).start()

    def all_sent(target, rows, send_sem, recv_sem):
        whole = pl.ds(0, (ND - 1) * rows)
        return pltpu.make_async_remote_copy(
            src_ref=target.at[whole],
            dst_ref=target.at[whole],
            send_sem=send_sem,
            recv_sem=recv_sem,
            device_id=device((me + 1) & (ND - 1)),
            device_id_type=MESH,
        )

    def rows_of(index, stride, count):
        return pl.ds(pl.multiple_of(index * stride, stride), count)

    def store_tiles(tiles, source, turn):
        block = (my_x + turn) & (NPX - 1)
        for j, tile in enumerate(tiles(block)):
            source[pl.ds(pl.multiple_of(256 * block + 16 * j, 16), 16), :] = tile.astype(BF16)

    def send_tiles(source, target, rows, turn, send_sem, recv_sem):
        mine = rows_of(me, 16, rows)
        block = (my_x + turn) & (NPX - 1)
        for j in range(1 if turn == 0 else 0, NPY):
            other = block * NPY + ((my_y + j) & (NPY - 1))
            send_one(source, target, mine, other, rows_of(other, 16, rows), send_sem, recv_sem)

    def keep_own(source, target, rows):
        mine = rows_of(me, 16, rows)
        target[mine, :] = source[mine, :]

    def first_tiles(block):
        tiles = swap_groups([mixed[block, level] for level in range(LEV)])
        lower = [tile_m[pl.ds(pl.multiple_of(128 * block + 8 * j, 8), 8), :] for j in range(16)]
        return [jnp.concatenate([tiles[j], lower[j]], axis=0) for j in range(16)]

    for turn in range(NPX):
        store_tiles(first_tiles, send_g, turn)
    send_tiles(send_g, recv_g, 16, 0, dense_send, dense_recv)
    pl.semaphore_wait(entered, NPX - 1)
    for turn in range(1, NPX):
        send_tiles(send_g, recv_g, 16, turn, dense_send, dense_recv)
    keep_own(send_g, recv_g, 16)
    dense = all_sent(recv_g, 16, dense_send, dense_recv)

    for load in loads[3:6]:
        load.wait()
    innov_wide[0:CH, :] = innov[...].astype(F32)

    def one_channel(channel, carry):
        values = jac[channel].astype(F32)
        scaled = values * w_ref[channel]
        low, high, rhs = carry
        rows = [jnp.broadcast_to(values[k : k + 1], (8, 128)) for k in range(LEV)]
        low = tuple(m + scaled[0:8] * rows[k] for k, m in enumerate(low))
        high = tuple(m + scaled[8:16] * rows[8 + k] for k, m in enumerate(high))
        return low, high, rhs + scaled * jnp.broadcast_to(innov_wide[pl.ds(channel, 1), :], (LEV, 128))

    def some_channels(index, carry):
        for k in range(8):
            carry = one_channel(8 * index + k, carry)
        return carry

    zero = jnp.zeros((8, 128), F32)
    carry = lax.fori_loop(
        0, CH // 8, some_channels, ((zero,) * LEV, (zero,) * 8, jnp.zeros((LEV, 128), F32))
    )
    for channel in range(CH // 8 * 8, CH):
        carry = one_channel(channel, carry)
    low, high, rhs = carry
    pack_high, pack_low = split(
        jnp.concatenate(list(low) + list(high) + [rhs, jnp.zeros((48, 128), F32)], axis=0)
    )
    packed = dot(chosen, pack_high, NT) + dot(chosen, pack_low, NT)
    for k in range(2):
        for i in range(2):
            send_m[pl.ds(2 * k + i, 128, stride=8), :] = packed[128 * k : 128 * k + 128, 128 * i : 128 * i + 128]
    own_rows = rows_of(me, 8, 4)

    def send_model(step):
        other = (me + step) & (ND - 1)
        send_one(send_m, recv_m, own_rows, other, rows_of(other, 8, 4), model_send, model_recv)

    @pl.loop(1, ND)
    def _(step):
        send_model(step)

    recv_m[own_rows, :] = send_m[own_rows, :]
    models = all_sent(recv_m, 4, model_send, model_recv)

    build_table(FY)

    dense.wait_recv()

    for block in range(8):
        values = recv_g[256 * block : 256 * block + 256, :].astype(F32).reshape(16, 16, 128)
        wide[128 * block : 128 * block + 128, :] = values[:, 8:16].reshape(128, 128)
        turned = jnp.transpose(values[:, 0:8].reshape(128, 128))
        grid[:, 8 * block : 8 * block + 8, :] = turned.reshape(LEV, 8, 128)

    for k in range(2):
        turned = jnp.transpose(wide[pl.ds(k, 128, stride=8), :])
        cell_x = turned[0:1] - 1.0
        cell_y = jnp.where(cell_x < 0.0, -1.0, 8.0 * turned[1:2] + turned[2:3])
        cells[k : k + 1, :] = cell_x
        cells[2 + k : 3 + k, :] = cell_y
    cells[4:8, :] = jnp.zeros((4, 128), F32)
    place[MIDDLE] = cells[...]

    def neighbour_copy(source, target, send_sem, recv_sem, slot):
        other = (me - (slot - MIDDLE)) & (ND - 1)
        return pltpu.make_async_remote_copy(
            src_ref=source,
            dst_ref=target.at[slot],
            send_sem=send_sem.at[slot],
            recv_sem=recv_sem.at[slot],
            device_id=device(other),
            device_id_type=MESH,
        )

    def for_neighbours(action, unroll=1):
        @pl.loop(0, NEAR - 1, unroll=unroll)
        def _(index):
            action(index + (index >= MIDDLE).astype(I32))

    for_neighbours(lambda slot: neighbour_copy(cells, place, cell_send, cell_recv, slot).start())

    def filter_to_field(level, own):
        out = along_y(own, FY, level)
        for b in range(8):
            high_field[8 * level : 8 * level + 8, 128 * b : 128 * b + 128] = out[8 * b : 8 * b + 8]

    for level in range(LEV):
        filter_to_field(level, grid[level])

    def both(slot, row):
        return jnp.concatenate([place[slot, row : row + 1, :], place[slot, row + 1 : row + 2, :]], axis=1)

    own_rows = both(MIDDLE, 2)
    row_number = iota((128, 256), 0).astype(F32)
    for block in range(8):
        hit = (row_number + float(128 * block)) == own_rows
        onehot_rows[128 * block : 128 * block + 128, :] = hit.astype(BF16)
    own_columns = both(MIDDLE, 0)
    own_column = jnp.broadcast_to(own_columns, (8, 256)) == iota((8, 256), 0).astype(F32)
    own_mask = jnp.broadcast_to(own_column[None], (LEV, 8, 256)).reshape(LEV * 8, 256)

    def sample():
        product = dot(stacked(high_field[...]), onehot_rows[...])
        product = product[:128] + product[128:]
        return jnp.sum(jnp.where(own_column[None], product.reshape(LEV, 8, 256), 0.0), axis=1)

    def apply_model(values):
        lower, upper = values[0:8], values[8:16]
        first = jnp.zeros((8, 256), F32)
        second = jnp.zeros((8, 256), F32)
        cross = []
        for k in range(LEV):
            first = first + model_low[k] * jnp.broadcast_to(values[k : k + 1], (8, 256))
        for k in range(8):
            second = second + model_high[k] * jnp.broadcast_to(upper[k : k + 1], (8, 256))
            cross.append(jnp.sum(model_low[8 + k] * lower, axis=0, keepdims=True))
        return jnp.concatenate([first, second + jnp.concatenate(cross, axis=0)], axis=0)

    z0 = sample()
    models.wait_recv()
    for k in range(2):
        lanes = slice(128 * k, 128 * k + 128)
        turned = jnp.transpose(recv_m[pl.ds(2 * k, 128, stride=8), :])
        model_low[:, :, lanes] = turned.reshape(LEV, 8, 128)
        turned = jnp.transpose(recv_m[pl.ds(2 * k + 1, 128, stride=8), :])
        model_high[:, :, lanes] = turned[0:64].reshape(8, 8, 128)
        extra[:, lanes] = turned[64:80]
    q1 = apply_model(z0) - extra[...]
    queue_a[...] = q1
    recv_a[MIDDLE] = q1
    for_neighbours(lambda slot: neighbour_copy(queue_a, recv_a, qa_send, qa_recv, slot).start())

    build_table(BY)
    build_table(BX)

    column = iota((8, 128), 1)
    offset = iota((8, 128), 0)

    @pl.loop(0, LEV, unroll=4)
    def _(level):
        taps = line[BX, pl.ds(level, 1), :]
        cov = dot(jnp.broadcast_to(taps, (8, 128)), circulant(taps), NT, precision=HIGHEST)
        ring = pltpu.roll(cov, 64, 1, stride=1, stride_axis=0)
        at = pl.ds(pl.multiple_of(8 * level, 8), 8)
        autocov[0, at, :] = jnp.where(column > offset, ring, 0.0)
        autocov[1, at, :] = jnp.where(column < offset, ring, 0.0)

    lane_number = iota((256, 128), 1).astype(F32)

    def build_onehot(slot):
        base = 256 * slot if isinstance(slot, int) else pl.multiple_of(256 * slot, 256)
        rows = place[slot]
        turned = jnp.transpose(jnp.concatenate([rows] + [jnp.zeros((8, 128), F32)] * 15, axis=0))
        rows_of = jnp.concatenate([turned[:, 2:3], turned[:, 3:4]], axis=0)
        rows_of = jnp.broadcast_to(rows_of, (256, 128))
        for block in range(8):
            hit = (lane_number + float(128 * block)) == rows_of
            onehot[pl.ds(base, 256), 128 * block : 128 * block + 128] = hit.astype(BF16)

        columns_of = both(slot, 0)
        wraps = slot == NEAR - 1
        first = jnp.where(wraps, 0, 8 * slot).astype(F32)
        hit = (row_number == columns_of + first).astype(BF16)
        product = dot(stacked(autocov[jnp.where(wraps, 1, 0)]), hit)
        near_x[slot] = product[:128] + product[128:]

    build_onehot(MIDDLE)

    def from_grid(then):
        for level in range(LEV):
            then(level, along_y(grid[level], BY, level))

    def to_grid(quarter, total):
        total = total[0:128] + total[128:256]
        for half in range(2):
            at = 16 * quarter + 8 * half
            grid[:, at : at + 8, :] = total[:, 128 * half : 128 * half + 128].reshape(LEV, 8, 128)

    def own_adjoint(index, values):
        def keep(level, out):
            adjoint[index, level] = out

        pair = stacked(jnp.where(own_mask, spread_levels(values), 0.0))
        for quarter in range(4):
            hits = onehot[256 * MIDDLE : 256 * MIDDLE + 256, 256 * quarter : 256 * quarter + 256]
            to_grid(quarter, dot(pair, hits))
        from_grid(keep)

    own_adjoint(0, q1)

    def arrive_cells(slot):
        neighbour_copy(cells, place, cell_send, cell_recv, slot).wait_recv()
        build_onehot(slot)

    for_neighbours(arrive_cells)

    groups = ((0, 4), (4, 9), (9, 13), (13, 17))

    def covary(source, target, send_sem, recv_sem, beside):
        for number, (first, last) in enumerate(groups):
            for slot in range(first, last):
                if slot != MIDDLE:
                    neighbour_copy(source, target, send_sem, recv_sem, slot).wait_recv()
                spread_q[:, 256 * slot : 256 * slot + 256] = stacked(near_x[slot] * spread_levels(target[slot]))
            for quarter in range(4):
                total = dot(
                    spread_q[:, 256 * first : 256 * last],
                    onehot[256 * first : 256 * last, 256 * quarter : 256 * quarter + 256],
                )
                if number:
                    total = total + field[quarter]
                if number == len(groups) - 1:
                    to_grid(quarter, total)
                else:
                    field[quarter] = total
            beside(number)
        from_grid(filter_to_field)
        return sample()

    t1 = covary(queue_a, recv_a, qa_send, qa_recv, lambda number: None)
    s0 = -(z0 + t1)
    q2 = apply_model(s0)
    queue_b[...] = q2
    recv_b[MIDDLE] = q2
    for_neighbours(lambda slot: neighbour_copy(queue_b, recv_b, qb_send, qb_recv, slot).start())
    own_adjoint(1, q2)

    def early_tiles(block):
        at = pl.ds(pl.multiple_of(8 * block, 8), 8)
        first, second = [
            swap_groups([adjoint[k, level, at, :] for level in range(LEV)]) for k in range(2)
        ]
        return [jnp.concatenate([first[j], second[j]], axis=0) for j in range(16)]

    def send_early(number):
        for turn in (2 * number, 2 * number + 1):
            send_tiles(send_f, recv_f, 16, turn, early_send, early_recv)

    for turn in range(NPX):
        store_tiles(early_tiles, send_f, turn)
    keep_own(send_f, recv_f, 16)
    lane = iota((1, 128), 1)

    def place_sums(row, first, values):
        for k, value in enumerate(values):
            row = jnp.where(lane == first + k, value, row)
        return row

    c0c0 = jnp.sum(jnp.sum(c0_ref[...] * c0_ref[...], axis=0))
    row = place_sums(
        jnp.zeros((1, 128), F32), 0, (c0c0, jnp.sum(z0 * q1), jnp.sum(q1 * t1), jnp.sum(s0 * q2))
    )
    t2 = covary(queue_b, recv_b, qb_send, qb_recv, send_early)
    early = all_sent(recv_f, 16, early_send, early_recv)
    u = apply_model(t2)

    own_adjoint(2, u)
    row = place_sums(row, 4, (jnp.sum(t2 * q2), jnp.sum(t2 * u)))

    for turn in range(NPX):
        block = (my_x + turn) & (NPX - 1)
        at = pl.ds(pl.multiple_of(8 * block, 8), 8)
        for j, tile in enumerate(swap_groups([adjoint[2, level, at, :] for level in range(LEV)])):
            send_u[pl.ds(pl.multiple_of(256 * block + 16 * j, 16), 8), :] = tile
            send_u[pl.ds(256 * block + 16 * j + 8, 1), :] = row
        send_tiles(send_u, recv_u, 9, turn, final_send, final_recv)
    keep_own(send_u, recv_u, 9)
    final = all_sent(recv_u, 9, final_send, final_recv)

    early.wait_recv()
    for block in range(8):
        arrived = recv_f[256 * block : 256 * block + 256, :].astype(F32).reshape(16, 2, 8, 128)
        for index in range(2):
            turned = jnp.transpose(arrived[:, index].reshape(128, 128))
            adjoint[index, :, 8 * block : 8 * block + 8, :] = turned.reshape(LEV, 8, 128)

    final.wait_recv()
    summed = jnp.sum(recv_u[pl.ds(8, ND, stride=16), :], axis=0, keepdims=True)
    c0c0, z0q1, q1t1, s0q2, q2t2, t2u = [summed[:, k : k + 1] for k in range(6)]
    norm0 = c0c0 + 2.0 * z0q1 + q1t1
    alpha0 = norm0 / (norm0 + s0q2)
    keep = 1.0 - alpha0
    norm1 = keep * keep * norm0 - 2.0 * alpha0 * keep * s0q2 + alpha0 * alpha0 * q2t2
    beta0 = norm1 / norm0
    gain = keep + beta0
    curvature = gain * gain * s0q2 - 2.0 * gain * alpha0 * q2t2 + alpha0 * alpha0 * t2u
    alpha1 = norm1 / (norm1 + beta0 * beta0 * norm0 + curvature)
    coef_c = alpha0 + alpha1 * gain
    coef_r = (1.0 - alpha1) * keep - alpha1 * beta0
    control_2 = alpha0 * alpha1
    residual_2 = (1.0 - alpha1) * alpha0 + alpha1 * gain
    residual_u = -alpha1 * alpha0

    for block in range(8):
        arrived = recv_u[256 * block : 256 * block + 256, :].reshape(16, 16, 128)[:, 0:8]
        turned = jnp.transpose(arrived.reshape(128, 128))
        adjoint[2, :, 8 * block : 8 * block + 8, :] = turned.reshape(LEV, 8, 128)

    for level in range(LEV):
        one, two, three = [adjoint[k, level] for k in range(3)]
        for index, coef, value in (
            (0, -coef_c, coef_c * one + control_2 * two),
            (1, 1.0 - coef_r, coef_r * one + residual_2 * two + residual_u * three),
        ):
            out = along_x(value, BX, level)
            for b in range(8):
                lanes = slice(128 * b, 128 * b + 128)
                change[index, level, :, lanes] = coef * c0_ref[level, :, lanes] - out[8 * b : 8 * b + 8]
            pltpu.make_async_copy(
                change.at[index, level], (control_hbm, residual_hbm)[index].at[level], store_sem.at[index]
            ).start()

    for index, target in enumerate((control_hbm, residual_hbm)):
        pltpu.make_async_copy(change.at[index], target, store_sem.at[index]).wait()

    dense.wait_send()
    models.wait_send()
    early.wait_send()
    final.wait_send()

    def sent(slot):
        neighbour_copy(cells, place, cell_send, cell_recv, slot).wait_send()
        neighbour_copy(queue_a, recv_a, qa_send, qa_recv, slot).wait_send()
        neighbour_copy(queue_b, recv_b, qb_send, qb_recv, slot).wait_send()

    for_neighbours(sent)


def per_device(
    control_init, kernel_x, kernel_y, obs_weight, jacobian, innovation, obs_dest, obs_cell
):
    anywhere = pl.BlockSpec(memory_space=pl.ANY)
    shape = jax.ShapeDtypeStruct(control_init.shape, F32)
    dma = pltpu.SemaphoreType.DMA
    change, shifted = pl.pallas_call(
        kernel,
        out_shape=(shape, shape),
        in_specs=[anywhere] * 8,
        out_specs=(anywhere, anywhere),
        scratch_shapes=[
            pltpu.VMEM((LEV, 8, 1024), F32),
            pltpu.VMEM((LEV, TAPS), F32),
            pltpu.VMEM((LEV, TAPS), F32),
            pltpu.SMEM((CH,), F32),
            pltpu.VMEM((CH, LEV, 128), BF16),
            pltpu.VMEM((CH, 128), BF16),
            pltpu.VMEM((1, 128), I32),
            pltpu.VMEM((1, 128), I32),
            pltpu.VMEM((CH + 1, 128), F32),
            pltpu.VMEM((4, LEV, 128), F32),
            pltpu.VMEM((4, LEV, 256, 256), BF16),
            pltpu.VMEM((8, LEV, 8, 128), F32),
            pltpu.VMEM((1024, 128), F32),
            pltpu.VMEM((2048, 128), BF16),
            pltpu.VMEM((2048, 128), BF16),
            pltpu.VMEM((1024, 128), F32),
            pltpu.VMEM((1024, 128), F32),
            pltpu.VMEM((1024, 128), F32),
            pltpu.VMEM((LEV, 8, 256), F32),
            pltpu.VMEM((8, 8, 256), F32),
            pltpu.VMEM((LEV, 256), F32),
            pltpu.VMEM((REACH, 1024), BF16),
            pltpu.VMEM((1024, 256), BF16),
            pltpu.VMEM((2, 128, 128), F32),
            pltpu.VMEM((NEAR, 128, 256), F32),
            pltpu.VMEM((NEAR, 8, 128), F32),
            pltpu.VMEM((8, 128), F32),
            pltpu.VMEM((LEV, 256), F32),
            pltpu.VMEM((LEV, 256), F32),
            pltpu.VMEM((NEAR, LEV, 256), F32),
            pltpu.VMEM((NEAR, LEV, 256), F32),
            pltpu.VMEM((256, REACH), BF16),
            pltpu.VMEM((LEV, 64, 128), F32),
            pltpu.VMEM((128, 1024), F32),
            pltpu.VMEM((3, LEV, 64, 128), F32),
            pltpu.VMEM((4, 256, 256), F32),
            pltpu.VMEM((2, LEV, 8, 1024), F32),
            pltpu.VMEM((2048, 128), F32),
            pltpu.VMEM((2048, 128), F32),
            pltpu.VMEM((2048, 128), BF16),
            pltpu.VMEM((2048, 128), BF16),
            pltpu.SemaphoreType.REGULAR,
            dma((8,)), dma((2,)),
            dma, dma, dma, dma,
            dma((NEAR,)), dma((NEAR,)),
            dma((NEAR,)), dma((NEAR,)), dma((NEAR,)), dma((NEAR,)),
            dma, dma, dma, dma,
        ],
        compiler_params=pltpu.CompilerParams(
            collective_id=0, has_side_effects=True, vmem_limit_bytes=60 * 1024 * 1024
        ),
    )(
        control_init,
        kernel_x,
        kernel_y,
        obs_weight,
        jnp.transpose(jacobian, (2, 1, 0)),
        jnp.transpose(innovation),
        jnp.transpose(obs_dest),
        obs_cell.reshape(1, -1),
    )
    return control_init + change, shifted - control_init


def solution(mesh):
    in_specs = (
        P(None, ("px", "py"), None),
        P(),
        P(),
        P(),
        P(("px", "py"), None, None),
        P(("px", "py"), None),
        P(("px", "py"), None),
        P(("px", "py")),
    )
    out_specs = (P(None, ("px", "py"), None), P(None, ("px", "py"), None))
    return jax.shard_map(
        per_device, mesh=mesh, in_specs=in_specs, out_specs=out_specs, check_vma=False
    )
```

```python
import functools

import jax
import jax.numpy as jnp
from jax import lax
from jax.experimental import pallas as pl
from jax.experimental.pallas import tpu as pltpu
from jax.sharding import PartitionSpec as P

F32, BF16, I32 = jnp.float32, jnp.bfloat16, jnp.int32
MESH = pl.DeviceIdType.MESH
ND, NPX, NPY = 128, 8, 16
LEV, CH, TAPS = 16, 431, 64
NEAR = 17
MIDDLE = 8
REACH = NEAR * 256
FX, BX, FY, BY = range(4)
NT = (((1,), (1,)), ((), ()))
NN = (((1,), (0,)), ((), ()))
HIGHEST = lax.Precision.HIGHEST


def iota(shape, axis):
    return lax.broadcasted_iota(I32, shape, axis)


def split(values):
    high = values.astype(BF16)
    low = (values - high.astype(F32)).astype(BF16)
    return high, low


def stacked(values):
    return jnp.concatenate(split(values), axis=0)


def dot(left, right, dims=NN, precision=None):
    return lax.dot_general(left, right, dims, precision=precision, preferred_element_type=F32)


def swap_groups(tiles):
    group = iota((8, 128), 1) // 8
    tiles = list(tiles)
    for bit in range(4):
        step = 1 << bit
        upper = (group & step) != 0
        for a in range(16):
            if a & step == 0:
                first, second = tiles[a], tiles[a + step]
                tiles[a] = jnp.where(upper, pltpu.roll(second, 8 * step, 1), first)
                tiles[a + step] = jnp.where(upper, second, pltpu.roll(first, 128 - 8 * step, 1))
    return tiles


def spread_levels(values):
    count = values.shape[1]
    return jnp.broadcast_to(values[:, None, :], (LEV, 8, count)).reshape(LEV * 8, count)


def kernel(
    c0_hbm, kx_hbm, ky_hbm, w_hbm, jac_hbm, innov_hbm, dest_hbm, cell_hbm,
    control_hbm, residual_hbm,
    c0_ref, kx_ref, ky_ref, w_ref, jac, innov, dest_ref, cell_ref,
    innov_wide, line, table, mixed, tile_m, send_g, recv_g, wide, send_m, recv_m,
    model_low, model_high, extra, onehot, onehot_rows, autocov, near_x, place, cells, queue_a, queue_b,
    recv_a, recv_b, spread_q, grid, high_field, adjoint, field, change, send_u, recv_u, send_f, recv_f,
    entered, load_sem, store_sem, model_send, model_recv, dense_send, dense_recv, cell_send, cell_recv,
    qa_send, qa_recv, qb_send, qb_recv, early_send, early_recv, final_send, final_recv,
):
    my_x, my_y = lax.axis_index("px"), lax.axis_index("py")
    me = my_x * NPY + my_y

    def device(index):
        return (index >> 4, index & 15)

    loads = [
        pltpu.make_async_copy(source, target, load_sem.at[i])
        for i, (source, target) in enumerate(
            (
                (c0_hbm, c0_ref), (kx_hbm, kx_ref), (ky_hbm, ky_ref), (w_hbm, w_ref),
                (jac_hbm, jac), (innov_hbm, innov), (dest_hbm, dest_ref), (cell_hbm, cell_ref),
            )
        )
    ]
    for load in loads:
        load.start()

    barrier = pltpu.get_barrier_semaphore()

    for step in range(1, NPY):
        pl.semaphore_signal(
            barrier, inc=1, device_id=(my_x, (my_y + step) & (NPY - 1)), device_id_type=MESH
        )
    for step in range(1, NPX):
        pl.semaphore_signal(
            barrier, inc=1, device_id=((my_x + step) & (NPX - 1), my_y), device_id_type=MESH
        )

    loads[1].wait()
    loads[2].wait()
    tap = iota((TAPS, 128), 0)
    place_at = iota((TAPS, 128), 1)
    pick_forward = (tap == ((32 - place_at) & 127)).astype(F32)
    pick_backward = (tap == ((place_at + 32) & 127)).astype(F32)
    for which, (taps_ref, pick) in enumerate(
        ((kx_ref, pick_forward), (kx_ref, pick_backward), (ky_ref, pick_forward), (ky_ref, pick_backward))
    ):
        line[which] = dot(taps_ref[...], pick, precision=HIGHEST)

    inside = jnp.abs(iota((128, 128), 0) - iota((128, 128), 1)) < 64

    def circulant(row):
        return pltpu.roll(jnp.broadcast_to(row, (128, 128)), 0, 1, stride=1, stride_axis=0)

    def build_table(which):
        @pl.loop(0, LEV, unroll=4)
        def _(level):
            ring = circulant(line[which, pl.ds(level, 1), :])
            high, low = split(ring)
            pair = jnp.concatenate([high, low], axis=1)
            nil = jnp.zeros((), BF16)
            keep = jnp.concatenate([inside, inside], axis=1)
            table[which, level, 0:128, :] = jnp.where(keep, pair, nil)
            table[which, level, 128:256, :] = jnp.where(keep, nil, pair)

    def convolve(own, before, after, which, level):
        count = own.shape[0]
        beside = jnp.where(iota((count, 128), 1) < 64, after, before)
        product = dot(stacked(jnp.concatenate([own, beside], axis=1)), table[which, level])
        upper, lower = product[:count], product[count:]
        return (upper[:, :128] + upper[:, 128:]) + (lower[:, :128] + lower[:, 128:])

    def along_x(own, which, level):
        before = jnp.concatenate([own[56:], own[:56]], axis=0)
        after = jnp.concatenate([own[8:], own[:8]], axis=0)
        return convolve(own, before, after, which, level)

    edge = jnp.zeros((8, 128), F32)

    def along_y(own, which, level):
        before = jnp.concatenate([edge, own[:56]], axis=0)
        after = jnp.concatenate([own[8:], edge], axis=0)
        return convolve(own, before, after, which, level)

    build_table(FX)
    loads[0].wait()

    for level in range(LEV):
        own = jnp.concatenate([c0_ref[level, :, 128 * b : 128 * b + 128] for b in range(8)], axis=0)
        out = along_x(own, FX, level)
        for b in range(8):
            mixed[b, level] = out[8 * b : 8 * b + 8]

    loads[6].wait()
    loads[7].wait()
    cell = cell_ref[...]
    codes = jnp.concatenate([(cell >> 10) + 1, (cell & 1023) >> 3, cell & 7, jnp.zeros((125, 128), I32)], axis=0)
    dest = jnp.broadcast_to(dest_ref[...], (128, 128))
    dest_t = jnp.transpose(dest.astype(F32))
    earlier = (dest.astype(F32) == dest_t) & (iota((128, 128), 0) < iota((128, 128), 1))
    rank = jnp.sum(earlier.astype(F32), axis=0, keepdims=True)
    named = iota((128, 128), 0) == dest
    chosen = jnp.concatenate([(named & (rank == float(k))).astype(BF16) for k in range(2)], axis=0)
    packed = dot(chosen, codes.astype(F32).astype(BF16), NT)
    for k in range(2):
        tile_m[pl.ds(k, 128, stride=8), :] = packed[128 * k : 128 * k + 128]
    for i in range(2, 8):
        tile_m[pl.ds(i, 128, stride=8), :] = jnp.zeros((128, 128), F32)

    pl.semaphore_wait(barrier, NPX + NPY - 2)
    for step in range(1, NPX):
        pl.semaphore_signal(
            entered, inc=1, device_id=((my_x + step) & (NPX - 1), my_y), device_id_type=MESH
        )
    def send_one(source, target, rows, other, source_rows, send_sem, recv_sem):
        pltpu.make_async_remote_copy(
            src_ref=source.at[source_rows],
            dst_ref=target.at[rows],
            send_sem=send_sem,
            recv_sem=recv_sem,
            device_id=device(other),
            device_id_type=MESH,
        ).start()

    def all_sent(target, rows, send_sem, recv_sem):
        whole = pl.ds(0, (ND - 1) * rows)
        return pltpu.make_async_remote_copy(
            src_ref=target.at[whole],
            dst_ref=target.at[whole],
            send_sem=send_sem,
            recv_sem=recv_sem,
            device_id=device((me + 1) & (ND - 1)),
            device_id_type=MESH,
        )

    def rows_of(index, stride, count):
        return pl.ds(pl.multiple_of(index * stride, stride), count)

    def store_tiles(tiles, source, turn):
        block = (my_x + turn) & (NPX - 1)
        for j, tile in enumerate(tiles(block)):
            source[pl.ds(pl.multiple_of(256 * block + 16 * j, 16), 16), :] = tile.astype(BF16)

    def send_tiles(source, target, rows, turn, send_sem, recv_sem):
        mine = rows_of(me, 16, rows)
        block = (my_x + turn) & (NPX - 1)
        for j in range(1 if turn == 0 else 0, NPY):
            other = block * NPY + ((my_y + j) & (NPY - 1))
            send_one(source, target, mine, other, rows_of(other, 16, rows), send_sem, recv_sem)

    def keep_own(source, target, rows):
        mine = rows_of(me, 16, rows)
        target[mine, :] = source[mine, :]

    def first_tiles(block):
        tiles = swap_groups([mixed[block, level] for level in range(LEV)])
        lower = [tile_m[pl.ds(pl.multiple_of(128 * block + 8 * j, 8), 8), :] for j in range(16)]
        return [jnp.concatenate([tiles[j], lower[j]], axis=0) for j in range(16)]

    for turn in range(NPX):
        store_tiles(first_tiles, send_g, turn)
    send_tiles(send_g, recv_g, 16, 0, dense_send, dense_recv)
    pl.semaphore_wait(entered, NPX - 1)
    for turn in range(1, NPX):
        send_tiles(send_g, recv_g, 16, turn, dense_send, dense_recv)
    keep_own(send_g, recv_g, 16)
    dense = all_sent(recv_g, 16, dense_send, dense_recv)

    for load in loads[3:6]:
        load.wait()
    innov_wide[...] = innov[...].astype(F32)

    def one_channel(channel, carry):
        values = jac[channel].astype(F32)
        scaled = values * w_ref[channel]
        low, high, rhs = carry
        rows = [jnp.broadcast_to(values[k : k + 1], (8, 128)) for k in range(LEV)]
        low = tuple(m + scaled[0:8] * rows[k] for k, m in enumerate(low))
        high = tuple(m + scaled[8:16] * rows[8 + k] for k, m in enumerate(high))
        return low, high, rhs + scaled * jnp.broadcast_to(innov_wide[pl.ds(channel, 1), :], (LEV, 128))

    def some_channels(index, carry):
        for k in range(8):
            carry = one_channel(8 * index + k, carry)
        return carry

    zero = jnp.zeros((8, 128), F32)
    carry = lax.fori_loop(
        0, CH // 8, some_channels, ((zero,) * LEV, (zero,) * 8, jnp.zeros((LEV, 128), F32))
    )
    for channel in range(CH // 8 * 8, CH):
        carry = one_channel(channel, carry)
    low, high, rhs = carry
    pack_high, pack_low = split(
        jnp.concatenate(list(low) + list(high) + [rhs, jnp.zeros((48, 128), F32)], axis=0)
    )
    packed = dot(chosen, pack_high, NT) + dot(chosen, pack_low, NT)
    for k in range(2):
        for i in range(2):
            send_m[pl.ds(2 * k + i, 128, stride=8), :] = packed[128 * k : 128 * k + 128, 128 * i : 128 * i + 128]
    own_rows = rows_of(me, 8, 4)

    def send_model(step):
        other = (me + step) & (ND - 1)
        send_one(send_m, recv_m, own_rows, other, rows_of(other, 8, 4), model_send, model_recv)

    @pl.loop(1, ND)
    def _(step):
        send_model(step)

    recv_m[own_rows, :] = send_m[own_rows, :]
    models = all_sent(recv_m, 4, model_send, model_recv)

    build_table(FY)
    build_table(BY)
    build_table(BX)

    column = iota((8, 128), 1)
    offset = iota((8, 128), 0)

    @pl.loop(0, LEV, unroll=4)
    def _(level):
        taps = line[BX, pl.ds(level, 1), :]
        cov = dot(jnp.broadcast_to(taps, (8, 128)), circulant(taps), NT, precision=HIGHEST)
        ring = pltpu.roll(cov, 64, 1, stride=1, stride_axis=0)
        at = pl.ds(pl.multiple_of(8 * level, 8), 8)
        autocov[0, at, :] = jnp.where(column > offset, ring, 0.0)
        autocov[1, at, :] = jnp.where(column < offset, ring, 0.0)

    dense.wait_recv()

    for block in range(8):
        values = recv_g[256 * block : 256 * block + 256, :].astype(F32).reshape(16, 16, 128)
        wide[128 * block : 128 * block + 128, :] = values[:, 8:16].reshape(128, 128)
        turned = jnp.transpose(values[:, 0:8].reshape(128, 128))
        grid[:, 8 * block : 8 * block + 8, :] = turned.reshape(LEV, 8, 128)

    for k in range(2):
        turned = jnp.transpose(wide[pl.ds(k, 128, stride=8), :])
        cell_x = turned[0:1] - 1.0
        cell_y = jnp.where(cell_x < 0.0, -1.0, 8.0 * turned[1:2] + turned[2:3])
        cells[k : k + 1, :] = cell_x
        cells[2 + k : 3 + k, :] = cell_y
    cells[4:8, :] = jnp.zeros((4, 128), F32)
    place[MIDDLE] = cells[...]

    def neighbour_copy(source, target, send_sem, recv_sem, slot):
        other = (me - (slot - MIDDLE)) & (ND - 1)
        return pltpu.make_async_remote_copy(
            src_ref=source,
            dst_ref=target.at[slot],
            send_sem=send_sem.at[slot],
            recv_sem=recv_sem.at[slot],
            device_id=device(other),
            device_id_type=MESH,
        )

    def for_neighbours(action, unroll=1):
        @pl.loop(0, NEAR - 1, unroll=unroll)
        def _(index):
            action(index + (index >= MIDDLE).astype(I32))

    for_neighbours(lambda slot: neighbour_copy(cells, place, cell_send, cell_recv, slot).start())

    def filter_to_field(level, own):
        out = along_y(own, FY, level)
        for b in range(8):
            high_field[8 * level : 8 * level + 8, 128 * b : 128 * b + 128] = out[8 * b : 8 * b + 8]

    for level in range(LEV):
        filter_to_field(level, grid[level])

    def both(slot, row):
        return jnp.concatenate([place[slot, row : row + 1, :], place[slot, row + 1 : row + 2, :]], axis=1)

    own_rows = both(MIDDLE, 2)
    row_number = iota((128, 256), 0).astype(F32)
    for block in range(8):
        hit = (row_number + float(128 * block)) == own_rows
        onehot_rows[128 * block : 128 * block + 128, :] = hit.astype(BF16)
    own_columns = both(MIDDLE, 0)
    own_column = jnp.broadcast_to(own_columns, (8, 256)) == iota((8, 256), 0).astype(F32)
    own_mask = jnp.broadcast_to(own_column[None], (LEV, 8, 256)).reshape(LEV * 8, 256)

    def sample():
        product = dot(stacked(high_field[...]), onehot_rows[...])
        product = product[:128] + product[128:]
        return jnp.sum(jnp.where(own_column[None], product.reshape(LEV, 8, 256), 0.0), axis=1)

    def apply_model(values):
        lower, upper = values[0:8], values[8:16]
        first = jnp.zeros((8, 256), F32)
        second = jnp.zeros((8, 256), F32)
        cross = []
        for k in range(LEV):
            first = first + model_low[k] * jnp.broadcast_to(values[k : k + 1], (8, 256))
        for k in range(8):
            second = second + model_high[k] * jnp.broadcast_to(upper[k : k + 1], (8, 256))
            cross.append(jnp.sum(model_low[8 + k] * lower, axis=0, keepdims=True))
        return jnp.concatenate([first, second + jnp.concatenate(cross, axis=0)], axis=0)

    z0 = sample()
    models.wait_recv()
    for k in range(2):
        lanes = slice(128 * k, 128 * k + 128)
        turned = jnp.transpose(recv_m[pl.ds(2 * k, 128, stride=8), :])
        model_low[:, :, lanes] = turned.reshape(LEV, 8, 128)
        turned = jnp.transpose(recv_m[pl.ds(2 * k + 1, 128, stride=8), :])
        model_high[:, :, lanes] = turned[0:64].reshape(8, 8, 128)
        extra[:, lanes] = turned[64:80]
    q1 = apply_model(z0) - extra[...]
    queue_a[...] = q1
    recv_a[MIDDLE] = q1
    for_neighbours(lambda slot: neighbour_copy(queue_a, recv_a, qa_send, qa_recv, slot).start())

    lane_number = iota((256, 128), 1).astype(F32)

    def build_onehot(slot):
        base = 256 * slot if isinstance(slot, int) else pl.multiple_of(256 * slot, 256)
        rows = place[slot]
        turned = jnp.transpose(jnp.concatenate([rows] + [jnp.zeros((8, 128), F32)] * 15, axis=0))
        rows_of = jnp.concatenate([turned[:, 2:3], turned[:, 3:4]], axis=0)
        rows_of = jnp.broadcast_to(rows_of, (256, 128))
        for block in range(8):
            hit = (lane_number + float(128 * block)) == rows_of
            onehot[pl.ds(base, 256), 128 * block : 128 * block + 128] = hit.astype(BF16)

        columns_of = both(slot, 0)
        wraps = slot == NEAR - 1
        first = jnp.where(wraps, 0, 8 * slot).astype(F32)
        hit = (row_number == columns_of + first).astype(BF16)
        product = dot(stacked(autocov[jnp.where(wraps, 1, 0)]), hit)
        near_x[slot] = product[:128] + product[128:]

    build_onehot(MIDDLE)

    def from_grid(then):
        for level in range(LEV):
            then(level, along_y(grid[level], BY, level))

    def to_grid(quarter, total):
        total = total[0:128] + total[128:256]
        for half in range(2):
            at = 16 * quarter + 8 * half
            grid[:, at : at + 8, :] = total[:, 128 * half : 128 * half + 128].reshape(LEV, 8, 128)

    def own_adjoint(index, values):
        def keep(level, out):
            adjoint[index, level] = out

        pair = stacked(jnp.where(own_mask, spread_levels(values), 0.0))
        for quarter in range(4):
            hits = onehot[256 * MIDDLE : 256 * MIDDLE + 256, 256 * quarter : 256 * quarter + 256]
            to_grid(quarter, dot(pair, hits))
        from_grid(keep)

    for_neighbours(lambda slot: neighbour_copy(cells, place, cell_send, cell_recv, slot).wait_recv())
    for_neighbours(build_onehot, unroll=2)

    groups = ((0, 4), (4, 9), (9, 13), (13, 17))

    def covary(source, target, send_sem, recv_sem, beside):
        for number, (first, last) in enumerate(groups):
            for slot in range(first, last):
                if slot != MIDDLE:
                    neighbour_copy(source, target, send_sem, recv_sem, slot).wait_recv()
                spread_q[:, 256 * slot : 256 * slot + 256] = stacked(near_x[slot] * spread_levels(target[slot]))
            for quarter in range(4):
                total = dot(
                    spread_q[:, 256 * first : 256 * last],
                    onehot[256 * first : 256 * last, 256 * quarter : 256 * quarter + 256],
                )
                if number:
                    total = total + field[quarter]
                if number == len(groups) - 1:
                    to_grid(quarter, total)
                else:
                    field[quarter] = total
            beside(number)
        from_grid(filter_to_field)
        return sample()

    t1 = covary(queue_a, recv_a, qa_send, qa_recv, lambda number: None)
    s0 = -(z0 + t1)
    q2 = apply_model(s0)
    queue_b[...] = q2
    recv_b[MIDDLE] = q2
    for_neighbours(lambda slot: neighbour_copy(queue_b, recv_b, qb_send, qb_recv, slot).start())
    own_adjoint(0, q1)
    own_adjoint(1, q2)

    def early_tiles(block):
        at = pl.ds(pl.multiple_of(8 * block, 8), 8)
        first, second = [
            swap_groups([adjoint[k, level, at, :] for level in range(LEV)]) for k in range(2)
        ]
        return [jnp.concatenate([first[j], second[j]], axis=0) for j in range(16)]

    def send_early(number):
        for turn in (2 * number, 2 * number + 1):
            send_tiles(send_f, recv_f, 16, turn, early_send, early_recv)

    for turn in range(NPX):
        store_tiles(early_tiles, send_f, turn)
    keep_own(send_f, recv_f, 16)
    lane = iota((1, 128), 1)

    def place_sums(row, first, values):
        for k, value in enumerate(values):
            row = jnp.where(lane == first + k, value, row)
        return row

    c0c0 = jnp.sum(jnp.sum(c0_ref[...] * c0_ref[...], axis=0))
    row = place_sums(
        jnp.zeros((1, 128), F32), 0, (c0c0, jnp.sum(z0 * q1), jnp.sum(q1 * t1), jnp.sum(s0 * q2))
    )
    t2 = covary(queue_b, recv_b, qb_send, qb_recv, send_early)
    early = all_sent(recv_f, 16, early_send, early_recv)
    u = apply_model(t2)

    own_adjoint(2, u)
    row = place_sums(row, 4, (jnp.sum(t2 * q2), jnp.sum(t2 * u)))

    for turn in range(NPX):
        block = (my_x + turn) & (NPX - 1)
        at = pl.ds(pl.multiple_of(8 * block, 8), 8)
        for j, tile in enumerate(swap_groups([adjoint[2, level, at, :] for level in range(LEV)])):
            send_u[pl.ds(pl.multiple_of(256 * block + 16 * j, 16), 8), :] = tile
            send_u[pl.ds(256 * block + 16 * j + 8, 1), :] = row
        send_tiles(send_u, recv_u, 9, turn, final_send, final_recv)
    keep_own(send_u, recv_u, 9)
    final = all_sent(recv_u, 9, final_send, final_recv)

    early.wait_recv()
    for block in range(8):
        arrived = recv_f[256 * block : 256 * block + 256, :].astype(F32).reshape(16, 2, 8, 128)
        for index in range(2):
            turned = jnp.transpose(arrived[:, index].reshape(128, 128))
            adjoint[index, :, 8 * block : 8 * block + 8, :] = turned.reshape(LEV, 8, 128)

    final.wait_recv()
    summed = jnp.sum(recv_u[pl.ds(8, ND, stride=16), :], axis=0, keepdims=True)
    c0c0, z0q1, q1t1, s0q2, q2t2, t2u = [summed[:, k : k + 1] for k in range(6)]
    norm0 = c0c0 + 2.0 * z0q1 + q1t1
    alpha0 = norm0 / (norm0 + s0q2)
    keep = 1.0 - alpha0
    norm1 = keep * keep * norm0 - 2.0 * alpha0 * keep * s0q2 + alpha0 * alpha0 * q2t2
    beta0 = norm1 / norm0
    gain = keep + beta0
    curvature = gain * gain * s0q2 - 2.0 * gain * alpha0 * q2t2 + alpha0 * alpha0 * t2u
    alpha1 = norm1 / (norm1 + beta0 * beta0 * norm0 + curvature)
    coef_c = alpha0 + alpha1 * gain
    coef_r = (1.0 - alpha1) * keep - alpha1 * beta0
    control_2 = alpha0 * alpha1
    residual_2 = (1.0 - alpha1) * alpha0 + alpha1 * gain
    residual_u = -alpha1 * alpha0

    for block in range(8):
        arrived = recv_u[256 * block : 256 * block + 256, :].reshape(16, 16, 128)[:, 0:8]
        turned = jnp.transpose(arrived.reshape(128, 128))
        adjoint[2, :, 8 * block : 8 * block + 8, :] = turned.reshape(LEV, 8, 128)

    for level in range(LEV):
        one, two, three = [adjoint[k, level] for k in range(3)]
        for index, coef, value in (
            (0, -coef_c, coef_c * one + control_2 * two),
            (1, 1.0 - coef_r, coef_r * one + residual_2 * two + residual_u * three),
        ):
            out = along_x(value, BX, level)
            for b in range(8):
                lanes = slice(128 * b, 128 * b + 128)
                change[index, level, :, lanes] = coef * c0_ref[level, :, lanes] - out[8 * b : 8 * b + 8]
            pltpu.make_async_copy(
                change.at[index, level], (control_hbm, residual_hbm)[index].at[level], store_sem.at[index]
            ).start()

    for index, target in enumerate((control_hbm, residual_hbm)):
        pltpu.make_async_copy(change.at[index], target, store_sem.at[index]).wait()

    dense.wait_send()
    models.wait_send()
    early.wait_send()
    final.wait_send()

    def sent(slot):
        neighbour_copy(cells, place, cell_send, cell_recv, slot).wait_send()
        neighbour_copy(queue_a, recv_a, qa_send, qa_recv, slot).wait_send()
        neighbour_copy(queue_b, recv_b, qb_send, qb_recv, slot).wait_send()

    for_neighbours(sent)


def per_device(
    control_init, kernel_x, kernel_y, obs_weight, jacobian, innovation, obs_dest, obs_cell
):
    anywhere = pl.BlockSpec(memory_space=pl.ANY)
    shape = jax.ShapeDtypeStruct(control_init.shape, F32)
    dma = pltpu.SemaphoreType.DMA
    change, shifted = pl.pallas_call(
        kernel,
        out_shape=(shape, shape),
        in_specs=[anywhere] * 8,
        out_specs=(anywhere, anywhere),
        scratch_shapes=[
            pltpu.VMEM((LEV, 8, 1024), F32),
            pltpu.VMEM((LEV, TAPS), F32),
            pltpu.VMEM((LEV, TAPS), F32),
            pltpu.SMEM((CH,), F32),
            pltpu.VMEM((CH, LEV, 128), BF16),
            pltpu.VMEM((CH, 128), BF16),
            pltpu.VMEM((1, 128), I32),
            pltpu.VMEM((1, 128), I32),
            pltpu.VMEM((CH, 128), F32),
            pltpu.VMEM((4, LEV, 128), F32),
            pltpu.VMEM((4, LEV, 256, 256), BF16),
            pltpu.VMEM((8, LEV, 8, 128), F32),
            pltpu.VMEM((1024, 128), F32),
            pltpu.VMEM((2048, 128), BF16),
            pltpu.VMEM((2048, 128), BF16),
            pltpu.VMEM((1024, 128), F32),
            pltpu.VMEM((1024, 128), F32),
            pltpu.VMEM((1024, 128), F32),
            pltpu.VMEM((LEV, 8, 256), F32),
            pltpu.VMEM((8, 8, 256), F32),
            pltpu.VMEM((LEV, 256), F32),
            pltpu.VMEM((REACH, 1024), BF16),
            pltpu.VMEM((1024, 256), BF16),
            pltpu.VMEM((2, 128, 128), F32),
            pltpu.VMEM((NEAR, 128, 256), F32),
            pltpu.VMEM((NEAR, 8, 128), F32),
            pltpu.VMEM((8, 128), F32),
            pltpu.VMEM((LEV, 256), F32),
            pltpu.VMEM((LEV, 256), F32),
            pltpu.VMEM((NEAR, LEV, 256), F32),
            pltpu.VMEM((NEAR, LEV, 256), F32),
            pltpu.VMEM((256, REACH), BF16),
            pltpu.VMEM((LEV, 64, 128), F32),
            pltpu.VMEM((128, 1024), F32),
            pltpu.VMEM((3, LEV, 64, 128), F32),
            pltpu.VMEM((4, 256, 256), F32),
            pltpu.VMEM((2, LEV, 8, 1024), F32),
            pltpu.VMEM((2048, 128), F32),
            pltpu.VMEM((2048, 128), F32),
            pltpu.VMEM((2048, 128), BF16),
            pltpu.VMEM((2048, 128), BF16),
            pltpu.SemaphoreType.REGULAR,
            dma((8,)), dma((2,)),
            dma, dma, dma, dma,
            dma((NEAR,)), dma((NEAR,)),
            dma((NEAR,)), dma((NEAR,)), dma((NEAR,)), dma((NEAR,)),
            dma, dma, dma, dma,
        ],
        compiler_params=pltpu.CompilerParams(
            collective_id=0, has_side_effects=True, vmem_limit_bytes=60 * 1024 * 1024
        ),
    )(
        control_init,
        kernel_x,
        kernel_y,
        obs_weight,
        jnp.transpose(jacobian, (2, 1, 0)),
        jnp.transpose(innovation),
        jnp.transpose(obs_dest),
        obs_cell.reshape(1, -1),
    )
    return control_init + change, shifted - control_init


def solution(mesh):
    in_specs = (
        P(None, ("px", "py"), None),
        P(),
        P(),
        P(),
        P(("px", "py"), None, None),
        P(("px", "py"), None),
        P(("px", "py"), None),
        P(("px", "py")),
    )
    out_specs = (P(None, ("px", "py"), None), P(None, ("px", "py"), None))
    return jax.shard_map(
        per_device, mesh=mesh, in_specs=in_specs, out_specs=out_specs, check_vma=False
    )
```
